256 devices in a mesh: aa: 32 (over y, x, z_hi), ga: 8 (over z_lo, core).
Axes of the slice: x: 4, y: 4, z: 8 (z_hi: 2, z_lo: 4; z = z_hi * 4 + z_lo), core: 2. Of those that a mesh axis runs over, the one named last changes fastest.
Arguments:
- activations: bfloat16 [256, 8192], P(None, 'ga'), may hold values from -6 to 6
- out_grads: bfloat16 [256, 28672], P(None, 'aa'), may hold values from -6 to 6
- train_acts: bfloat16 [256, 8192], P(None, 'ga'), may hold values from -6 to 6
- train_grads: bfloat16 [256, 28672], P(None, 'aa'), may hold values from -6 to 6
- basis_in: bfloat16 [8192, 8192], P('ga', 'aa'), may hold values from -0.0625 to 0.0625
- basis_out: bfloat16 [28672, 28672], P('aa', 'ga'), may hold values from -0.03125 to 0.03125
- eigen_diag: bfloat16 [28672, 8192], P('ga', 'aa'), may hold values from 4 to 64
- damp_grid: float32 [16], replicated, may hold values from 0.5 to 8
- damp_pick: int32 [2], replicated, may hold values from 0 to 15
Outputs:
- scores: float32 [2, 256], replicated
The draws below stay inside these ranges and needn't reach their ends.
Inputs may be any that keep to these rules, and one draw needn't show every extreme that they name: `damp_pick`: indices into damp_grid.
All inputs are finite; a program needn't handle non-finite values.
Results may differ from the reference program's by a relative error of at most 0.0054.
Values may be sent and summed in bfloat16 or wider, within the bound.
No kernel may reach another device: no remote copies, remote signals or barrier semaphores. Data moves between devices by JAX's collectives and lax.ppermute only.
A program may use at most 64 MiB of HBM per device.

```python
import math
import jax
import jax.numpy as jnp
from jax import lax

D_IN = 8192
D_OUT = 28672
TOK_SEQ = 128
SEQS = 2
TRAIN_SEQS = 2
NDAMP = 16


def steps_of(stream_key, dims, pieces, least, largest):
    gain, own = 1.0, jax.random.fold_in(stream_key, 6)
    for axis_at, shards_of in pieces:
        heights = jnp.exp(jax.random.uniform(jax.random.fold_in(own, axis_at), (shards_of,), jnp.float32, least / len(pieces), largest / len(pieces)))
        gain = gain * jnp.repeat(heights, dims[axis_at] // shards_of).reshape([-1 if axis == axis_at else 1 for axis in range(len(dims))])
    return gain


def centred(stream_key, shape, scale, limit, split=(), kind=jnp.bfloat16):
    factor_of = steps_of(stream_key, shape, split, -0.22, 0.18) if split else 1.0
    entries = jax.random.normal(stream_key, shape, jnp.float32) * scale * factor_of
    return jnp.minimum(jnp.maximum(entries, -limit), limit).astype(kind)


def setup_inputs(seed: int = 0) -> dict:
    streams_of = jax.random.split(jax.random.key(seed), 10)
    activations = centred(streams_of[0], (SEQS * TOK_SEQ, D_IN), 1.0, 6.0, ((1, 8),))
    out_grads = centred(streams_of[1], (SEQS * TOK_SEQ, D_OUT), 1.0, 6.0, ((1, 32),))
    train_acts = centred(streams_of[2], (TRAIN_SEQS * TOK_SEQ, D_IN), 1.0, 6.0, ((1, 8),))
    train_grads = centred(streams_of[3], (TRAIN_SEQS * TOK_SEQ, D_OUT), 1.0, 6.0, ((1, 32),))
    basis_in = centred(streams_of[4], (D_IN, D_IN), D_IN ** -0.5, 0.0625, ((0, 8), (1, 32)))
    basis_out = centred(streams_of[5], (D_OUT, D_OUT), D_OUT ** -0.5, 0.03125, ((0, 32), (1, 8)))
    eigen_diag = jnp.clip(jnp.exp(math.log(64.0) - 2.7725887 * jax.random.uniform(streams_of[6], (D_OUT, D_IN), jnp.float32) ** steps_of(streams_of[6], (D_OUT, D_IN), ((0, 8), (1, 32)), -0.2, 0.2)), 4.0, 64.0).astype(jnp.bfloat16)
    damp_grid = jnp.clip(jnp.exp(jax.random.uniform(streams_of[7], (NDAMP,), jnp.float32, math.log(0.5), math.log(8.0))), 0.5, 8.0)
    damp_pick = jax.random.randint(streams_of[8], (SEQS,), 0, NDAMP).astype(jnp.int32)
    return {"activations": activations, "out_grads": out_grads, "train_acts": train_acts, "train_grads": train_grads, "basis_in": basis_in, "basis_out": basis_out, "eigen_diag": eigen_diag, "damp_grid": damp_grid, "damp_pick": damp_pick}


def reference(activations, out_grads, train_acts, train_grads, basis_in, basis_out, eigen_diag, damp_grid, damp_pick):
    rot_in = jnp.dot(activations, basis_in, preferred_element_type=jnp.float32).astype(jnp.bfloat16)
    train_in = jnp.dot(train_acts, basis_in, preferred_element_type=jnp.float32).astype(jnp.bfloat16)
    rot_out = jnp.dot(out_grads, basis_out, preferred_element_type=jnp.float32).astype(jnp.bfloat16)
    train_out = jnp.dot(train_grads, basis_out, preferred_element_type=jnp.float32).astype(jnp.bfloat16)
    train_cols = train_out.astype(jnp.float32).T
    diag_values = eigen_diag.astype(jnp.float32)
    grid_index = jnp.arange(NDAMP, dtype=jnp.int32)
    factor = 1.0 / math.sqrt(D_IN * D_OUT)

    def one_seq(index_seq):
        first = (index_seq * TOK_SEQ).astype(jnp.int32)
        in_rows = lax.dynamic_slice_in_dim(rot_in, first, TOK_SEQ, 0)
        out_rows = lax.dynamic_slice_in_dim(rot_out, first, TOK_SEQ, 0)
        rotated = lax.dot_general(out_rows, in_rows, (((0,), (0,)), ((), ())), preferred_element_type=jnp.float32)
        pick_seq = lax.dynamic_slice_in_dim(damp_pick, index_seq, 1, 0)
        damping = jnp.sum(jnp.where(pick_seq == grid_index, damp_grid, jnp.zeros_like(damp_grid)))
        precond = (rotated / (diag_values + damping)).astype(jnp.bfloat16)
        weighted = lax.dot_general(precond, train_in, (((1,), (1,)), ((), ())), preferred_element_type=jnp.float32)
        return lax.optimization_barrier(jnp.sum(weighted * train_cols, axis=0)) * factor
    return lax.map(one_seq, jnp.arange(SEQS, dtype=jnp.int32))
```

```python
import functools
import itertools
import math

import jax
import jax.numpy as jnp
from jax import lax
from jax.experimental import pallas as pl
from jax.experimental.pallas import tpu as pltpu
from jax.sharding import Mesh, PartitionSpec as P

D_IN = 8192
D_OUT = 28672
SIZES = (4, 4, 2, 4, 2)
ALL = ("y", "x", "zh", "zl", "c")
SCALE = 1.0 / math.sqrt(D_IN * D_OUT)
BF = jnp.bfloat16
F32 = jnp.float32
VLIM = 56 * 1024 * 1024


def flat(place):
    n = 0
    for size, at in zip(SIZES, place):
        n = n * size + at
    return n


def shift(k, first):
    pairs = []
    for y, x, zh, zl, c in itertools.product(*(range(s) for s in SIZES)):
        if (c == 0) == first:
            to = (y, (x + k) % 4, zh, zl, c)
        else:
            to = ((y + k) % 4, x, zh, zl, c)
        pairs.append((flat((y, x, zh, zl, c)), flat(to)))
    return pairs


FIRST = {k: shift(k, True) for k in (1, 2, 3)}
SECOND = {k: shift(k, False) for k in (1, 2, 3)}
HOPS = (2, 1, 3)


def move(value, pairs):
    return lax.ppermute(value, ALL, pairs)


def params():
    return pltpu.CompilerParams(vmem_limit_bytes=VLIM)


def mm_kernel(at, q_ref, t_ref, b_ref, o_ref):
    half = q_ref.shape[0]
    o_ref[:half] = jnp.dot(q_ref[...], b_ref[...], preferred_element_type=F32).astype(o_ref.dtype)
    o_ref[half:] = jnp.dot(t_ref[...], b_ref[...], preferred_element_type=F32).astype(o_ref.dtype)


def block_mm(q, t, basis, block, width, dtype):
    rows, depth = q.shape
    whole = pl.BlockSpec((rows, depth), lambda i, at: (0, 0))
    return pl.pallas_call(
        mm_kernel,
        grid_spec=pltpu.PrefetchScalarGridSpec(
            num_scalar_prefetch=1,
            grid=(1,),
            in_specs=[whole, whole, pl.BlockSpec((depth, width), lambda i, at: (0, at[0]))],
            out_specs=pl.BlockSpec((2 * rows, width), lambda i, at: (0, 0)),
        ),
        out_shape=jax.ShapeDtypeStruct((2 * rows, width), dtype),
        compiler_params=params(),
    )(block.reshape(1), q, t, basis)


def pick_kernel(at, *refs):
    half = len(refs) // 2
    for src, dst in zip(refs[:half], refs[half:]):
        dst[...] = src[...]


def pick_blocks(array, me, rows):
    cols = array.shape[1]
    return pl.pallas_call(
        pick_kernel,
        grid_spec=pltpu.PrefetchScalarGridSpec(
            num_scalar_prefetch=1,
            grid=(1,),
            in_specs=[
                pl.BlockSpec((rows, cols), lambda i, at, k=k: (lax.rem(at[0] + k, 4), 0)) for k in (0, *HOPS)
            ],
            out_specs=[pl.BlockSpec((rows, cols), lambda i, at: (0, 0))] * 4,
        ),
        out_shape=[jax.ShapeDtypeStruct((rows, cols), array.dtype)] * 4,
        compiler_params=params(),
    )(me.reshape(1), array, array, array, array)


def sum_kernel(at, own, a, b, c, o2, o1, o3, keep):
    i = pl.program_id(0)
    total = own[...] + a[...].astype(F32) + b[...].astype(F32) + c[...].astype(F32)
    for n, dst in enumerate((o2, o1, o3)):

        @pl.when(i == n)
        def _():
            dst[...] = total.astype(BF)

    @pl.when(i == 3)
    def _():
        keep[...] = total


def sum_blocks(own, parts, me):
    rows, cols = own.shape
    part = rows // 4

    def at_block(i, at):
        hop = jnp.where(i == 0, 2, jnp.where(i == 1, 1, jnp.where(i == 2, 3, 0)))
        return (lax.rem(at[0] + hop, 4), 0)

    fixed = pl.BlockSpec((part, cols), lambda i, at: (0, 0))
    small = jax.ShapeDtypeStruct((part, cols), BF)
    return pl.pallas_call(
        sum_kernel,
        grid_spec=pltpu.PrefetchScalarGridSpec(
            num_scalar_prefetch=1,
            grid=(4,),
            in_specs=[pl.BlockSpec((part, cols), at_block)] * 4,
            out_specs=[fixed] * 4,
        ),
        out_shape=[small, small, small, jax.ShapeDtypeStruct((part, cols), F32)],
        compiler_params=params(),
    )(me.reshape(1), own, *parts)


def score_kernel(me, pick, grid, p0, p2, p1, p3, e0, e2, e1, e3, r0, r2, r1, r3, out, rot, rot_t, ti_t):
    part = p0.shape[0]
    for k, piece in ((0, p0), (2, p2), (1, p1), (3, p3)):
        row = pl.multiple_of(lax.rem(me[0] + 4 - k, 4) * part, part)
        rot[pl.ds(row, part), :] = piece[...]
    eigs = (e0, e2, e1, e3)
    ins = (r0, r2, r1, r3)
    for n, r in enumerate(ins):
        ti_t[n] = r[256:, :].T
    for n in range(rot.shape[1] // 128):
        rot_t[n * 128 : (n + 1) * 128, :] = rot[:, n * 128 : (n + 1) * 128].T
    damp = [grid[pick[s]] for s in range(2)]

    def chunk(n, sums):
        rows = pl.ds(pl.multiple_of(n * 128, 128), 128)
        weights = [None, None]
        for k in range(4):
            diag = eigs[k][rows, :].astype(F32)
            for s in range(2):
                rotated = jnp.dot(
                    rot_t[rows, s * 128 : (s + 1) * 128],
                    ins[k][s * 128 : (s + 1) * 128, :],
                    preferred_element_type=F32,
                )
                precond = (rotated / (diag + damp[s])).astype(BF)
                w = jnp.dot(precond, ti_t[k], preferred_element_type=F32)
                weights[s] = w if weights[s] is None else weights[s] + w
        train = rot_t[rows, 256:].astype(F32)
        return tuple(
            sums[s] + jnp.sum((weights[s] * train).reshape(16, 8, 256), axis=0) for s in range(2)
        )

    zero = jnp.zeros((8, 256), F32)
    sums = lax.fori_loop(0, rot.shape[1] // 128, chunk, (zero, zero))
    both = jnp.concatenate([jnp.sum(v, axis=0, keepdims=True) for v in sums], axis=0) * SCALE
    out[...] = jnp.broadcast_to(both[None], out.shape)


def score(me, pick, grid, pieces, eigs, ins):
    tokens, cols = pieces[0].shape
    smem = pl.BlockSpec(memory_space=pltpu.SMEM)
    vmem = pl.BlockSpec(memory_space=pltpu.VMEM)
    return pl.pallas_call(
        score_kernel,
        in_specs=[smem] * 3 + [vmem] * 12,
        out_specs=vmem,
        out_shape=jax.ShapeDtypeStruct((16, 2, 256), F32),
        scratch_shapes=[
            pltpu.VMEM((4 * tokens, cols), BF),
            pltpu.VMEM((cols, 4 * tokens), BF),
            pltpu.VMEM((4, 256, 256), BF),
        ],
        compiler_params=params(),
    )(me.reshape(1), pick, grid, *pieces, *eigs, *ins)


def body(acts, out_grads, train_acts, train_grads, basis_in, basis_out, eig, grid, pick):
    y, x, c = lax.axis_index("y"), lax.axis_index("x"), lax.axis_index("c")
    first = jnp.where(c == 0, x, y).astype(jnp.int32)
    second = jnp.where(c == 0, y, x).astype(jnp.int32)
    zero = jnp.zeros((), jnp.int32)
    width = basis_out.shape[1] // 4

    got = []
    for k in HOPS:
        part = block_mm(out_grads, train_grads, basis_out, lax.rem(first + k, 4), width, BF)
        got.append(move(part, FIRST[k]))
    own = block_mm(out_grads, train_grads, basis_out, first, width, F32)
    in_part = block_mm(acts, train_acts, basis_in, zero, basis_in.shape[1], F32)

    split = lax.all_to_all(in_part, ("zl", "c"), 0, 0, tiled=True)
    rows = split.shape[0] // 8
    in_rows = jnp.sum(split.reshape(8, rows, -1), axis=0).astype(BF)
    spread = jnp.broadcast_to(in_rows[None], (8, *in_rows.shape))
    rot_in = lax.all_to_all(spread, ("zl", "c"), 0, 0, tiled=True).reshape(8 * rows, -1)

    s2, s1, s3, keep = sum_blocks(own, got, second)
    got2 = [move(v, SECOND[k]) for k, v in zip(HOPS, (s2, s1, s3))]
    eig_own, *eig_send = pick_blocks(eig, first, width)
    rot_in, *eig_send = lax.optimization_barrier((rot_in, *eig_send, s2))[:4]
    eigs = [eig_own] + [move(v, FIRST[k]) for k, v in zip(HOPS, eig_send)]
    ins = [rot_in] + [move(rot_in, FIRST[k]) for k in HOPS]
    total = keep
    for v in got2:
        total = total + v.astype(F32)
    other = lax.ppermute(total.astype(BF), "zh", [(0, 1), (1, 0)])
    total = (total + other.astype(F32)).astype(BF)
    pieces = [total] + [move(total, SECOND[k]) for k in HOPS]

    part = score(second, pick, grid, pieces, eigs, ins)
    over = jnp.sum(lax.all_to_all(part, ("y", "x"), 0, 0, tiled=True), axis=0)
    over = jnp.broadcast_to(over[None], (16, *over.shape))
    return jnp.sum(lax.all_to_all(over, ("zh", "zl", "c"), 0, 0, tiled=True), axis=0)


def solution(mesh):
    fine = Mesh(mesh.devices.reshape(SIZES), ALL)
    aa, ga = ("y", "x", "zh"), ("zl", "c")
    return jax.shard_map(
        body,
        mesh=fine,
        in_specs=(
            P(None, ga),
            P(None, aa),
            P(None, ga),
            P(None, aa),
            P(ga, aa),
            P(aa, ga),
            P(ga, aa),
            P(),
            P(),
        ),
        out_specs=P(),
        check_vma=False,
    )
```

```python
import functools
import itertools
import math

import jax
import jax.numpy as jnp
from jax import lax
from jax.experimental import pallas as pl
from jax.experimental.pallas import tpu as pltpu
from jax.sharding import Mesh, PartitionSpec as P

D_IN = 8192
D_OUT = 28672
SIZES = (4, 4, 2, 4, 2)
ALL = ("y", "x", "zh", "zl", "c")
SCALE = 1.0 / math.sqrt(D_IN * D_OUT)
BF = jnp.bfloat16
F32 = jnp.float32
MIB = 1024 * 1024


def flat(place):
    n = 0
    for size, at in zip(SIZES, place):
        n = n * size + at
    return n


def shift(k, first):
    pairs = []
    for y, x, zh, zl, c in itertools.product(*(range(s) for s in SIZES)):
        if (c == 0) == first:
            to = (y, (x + k) % 4, zh, zl, c)
        else:
            to = ((y + k) % 4, x, zh, zl, c)
        pairs.append((flat((y, x, zh, zl, c)), flat(to)))
    return pairs


FIRST = {k: shift(k, True) for k in (1, 2, 3)}
SECOND = {k: shift(k, False) for k in (1, 2, 3)}
HOPS = (2, 1, 3)


def move(value, pairs):
    return lax.ppermute(value, ALL, pairs)


def params(mib, us):
    return {
        "compiler_params": pltpu.CompilerParams(vmem_limit_bytes=mib * MIB),
        "cost_estimate": pl.CostEstimate(flops=int(us * 1.15e9), bytes_accessed=0, transcendentals=0),
    }


SMEM = pl.BlockSpec(memory_space=pltpu.SMEM)
VMEM = pl.BlockSpec(memory_space=pltpu.VMEM)


def lead_kernel(hops, at, q_hbm, t_hbm, b_hbm, *refs):
    outs, (q, t, b, sems) = refs[: 2 * len(hops)], refs[2 * len(hops) :]
    width = outs[0].shape[1]
    loads = [pltpu.make_async_copy(q_hbm, q, sems.at[0]), pltpu.make_async_copy(t_hbm, t, sems.at[1])]
    for n, k in enumerate(hops):
        cols = pl.ds(pl.multiple_of(lax.rem(at[0] + k, 4) * width, width), width)
        loads.append(pltpu.make_async_copy(b_hbm.at[:, cols], b.at[n], sems.at[2 + n]))
    for n in (0, 2, 1, *range(3, len(loads))):
        loads[n].start()
    for n in range(len(hops)):
        loads[2 + n].wait()
        for m, rows in enumerate((q, t)):
            if n == 0:
                loads[m].wait()
            dst = outs[2 * n + m]
            dst[...] = jnp.dot(rows[...], b[n], preferred_element_type=F32).astype(dst.dtype)


def lead_mm(q, t, basis, me, hops, width):
    rows, depth = q.shape
    hbm = pl.BlockSpec(memory_space=pltpu.HBM)
    return pl.pallas_call(
        functools.partial(lead_kernel, hops),
        in_specs=[SMEM, hbm, hbm, hbm],
        out_specs=[VMEM] * (2 * len(hops)),
        out_shape=[jax.ShapeDtypeStruct((rows, width), BF)] * (2 * len(hops)),
        scratch_shapes=[
            pltpu.VMEM((rows, depth), BF),
            pltpu.VMEM((rows, depth), BF),
            pltpu.VMEM((len(hops), depth, width), BF),
            pltpu.SemaphoreType.DMA((2 + len(hops),)),
        ],
        **params(58, 5),
    )(me.reshape(1), q, t, basis)


def open_kernel(at, core_at, q_hbm, t_hbm, b_hbm, aq_hbm, at_hbm, bi_hbm, oq, ot, mine, other, q, t, b, aq, ta, bi, sems):
    width = oq.shape[1]
    cols = pl.ds(pl.multiple_of(lax.rem(at[0] + 2, 4) * width, width), width)
    pairs = ((aq_hbm, aq), (at_hbm, ta), (bi_hbm, bi), (q_hbm, q), (b_hbm.at[:, cols], b), (t_hbm, t))
    loads = [pltpu.make_async_copy(src, dst, sems.at[n]) for n, (src, dst) in enumerate(pairs)]
    for load in loads:
        load.start()
    for load in loads[:3]:
        load.wait()
    for core in range(2):

        @pl.when(core_at[0] == core)
        def _():
            mine[...] = jnp.dot((aq, ta)[core][...], bi[...], preferred_element_type=F32)
            other[...] = jnp.dot((ta, aq)[core][...], bi[...], preferred_element_type=F32)

    loads[3].wait()
    loads[4].wait()
    oq[...] = jnp.dot(q[...], b[...], preferred_element_type=F32).astype(oq.dtype)
    loads[5].wait()
    ot[...] = jnp.dot(t[...], b[...], preferred_element_type=F32).astype(ot.dtype)


def open_mm(first, core, grads, basis_out, acts, basis_in, width):
    (rows, depth), (in_depth, in_width) = grads[0].shape, basis_in.shape
    hbm = pl.BlockSpec(memory_space=pltpu.HBM)
    return pl.pallas_call(
        open_kernel,
        in_specs=[SMEM] * 2 + [hbm] * 6,
        out_specs=[VMEM] * 4,
        out_shape=[jax.ShapeDtypeStruct((rows, width), BF)] * 2 + [jax.ShapeDtypeStruct((rows, in_width), F32)] * 2,
        scratch_shapes=[
            pltpu.VMEM((rows, depth), BF),
            pltpu.VMEM((rows, depth), BF),
            pltpu.VMEM((depth, width), BF),
            pltpu.VMEM((rows, in_depth), BF),
            pltpu.VMEM((rows, in_depth), BF),
            pltpu.VMEM((in_depth, in_width), BF),
            pltpu.SemaphoreType.DMA((6,)),
        ],
        **params(58, 4.5),
    )(first.reshape(1), core.reshape(1), *grads, basis_out, *acts, basis_in)


def mm_kernel(hops, at, q_ref, t_ref, b_ref, *outs):
    width = outs[0].shape[1]
    blocks = b_ref.shape[1] // width
    for n, k in enumerate(hops):
        if blocks == 1:
            basis = b_ref[...]
        else:
            basis = b_ref[:, pl.ds(pl.multiple_of(lax.rem(at[0] + k, blocks) * width, width), width)]
        for ref, dst in ((q_ref, outs[2 * n]), (t_ref, outs[2 * n + 1])):
            dst[...] = jnp.dot(ref[...], basis, preferred_element_type=F32).astype(dst.dtype)


def block_mm(q, t, basis, me, hops, width, dtypes):
    return pl.pallas_call(
        functools.partial(mm_kernel, hops),
        in_specs=[SMEM, VMEM, VMEM, VMEM],
        out_specs=[VMEM] * (2 * len(hops)),
        out_shape=[jax.ShapeDtypeStruct((q.shape[0], width), d) for d in dtypes for _ in range(2)],
        **params(20, 4),
    )(me.reshape(1), q, t, basis)


def pick_kernel(at, *refs):
    half = len(refs) // 2
    for src, dst in zip(refs[:half], refs[half:]):
        dst[...] = src[...]


def pick_blocks(array, me, rows):
    cols = array.shape[1]
    return pl.pallas_call(
        pick_kernel,
        grid_spec=pltpu.PrefetchScalarGridSpec(
            num_scalar_prefetch=1,
            grid=(1,),
            in_specs=[
                pl.BlockSpec((rows, cols), lambda i, at, k=k: (lax.rem(at[0] + k, 4), 0)) for k in (0, *HOPS)
            ],
            out_specs=[pl.BlockSpec((rows, cols), lambda i, at: (0, 0))] * 4,
        ),
        out_shape=[jax.ShapeDtypeStruct((rows, cols), array.dtype)] * 4,
        **params(16, 1.2),
    )(me.reshape(1), array, array, array, array)


def sum_kernel(at, own_q, own_t, q1, q2, t1, t2, o2, o1, o3, keep):
    part = keep.shape[0] // 2
    for hop, dst in ((2, o2), (1, o1), (3, o3), (0, keep)):
        rows = pl.ds(pl.multiple_of(lax.rem(at[0] + hop, 4) * part, part), part)
        for n, (a, b, c) in enumerate(((own_q, q1, q2), (own_t, t1, t2))):
            total = a[rows, :] + b[rows, :].astype(F32) + c[rows, :].astype(F32)
            dst[n * part : (n + 1) * part, :] = total.astype(dst.dtype)


def sum_blocks(me, *parts):
    rows, cols = parts[0].shape
    small = jax.ShapeDtypeStruct((rows // 2, cols), BF)
    return pl.pallas_call(
        sum_kernel,
        in_specs=[SMEM] + [VMEM] * 6,
        out_specs=[VMEM] * 4,
        out_shape=[small, small, small, jax.ShapeDtypeStruct((rows // 2, cols), F32)],
        **params(12, 1.6),
    )(me.reshape(1), *parts)


def gather_rows(me, pieces, whole):
    part = pieces[0].shape[0] // 2
    for k, piece in zip((0, *HOPS), pieces):
        row = lax.rem(me[0] + 4 - k, 4) * part
        whole[pl.ds(pl.multiple_of(row, part), part), :] = piece[:part, :]
        whole[pl.ds(pl.multiple_of(row + 4 * part, part), part), :] = piece[part:, :]


def add_kernel(*refs):
    *parts, out = refs
    total = parts[0][...].astype(F32)
    for part in parts[1:]:
        total = total + part[...].astype(F32)
    out[...] = total.astype(out.dtype)


def add(dtype, *parts, us=0.1):
    return pl.pallas_call(
        add_kernel,
        in_specs=[VMEM] * len(parts),
        out_specs=VMEM,
        out_shape=jax.ShapeDtypeStruct(parts[0].shape, dtype),
        **params(8, us),
    )(*parts)


def pack_kernel(at, mine, other, e2, e1, e3, o2, o1, o3, rot_in):
    part = mine.shape[0]
    rot_in[pl.ds(pl.multiple_of(at[0] * part, part), part), :] = mine[...]
    rot_in[pl.ds(pl.multiple_of((1 - at[0]) * part, part), part), :] = other[...]
    rows = e2.shape[0]
    for src, dst in ((e2, o2), (e1, o1), (e3, o3)):
        dst[:rows, :] = src[...]
        dst[rows:, :] = rot_in[...]


def pack(me, mine, other, eigs):
    rows, cols = mine.shape
    both = jax.ShapeDtypeStruct((eigs[0].shape[0] + 2 * rows, cols), mine.dtype)
    return pl.pallas_call(
        pack_kernel,
        in_specs=[SMEM] + [VMEM] * 5,
        out_specs=[VMEM] * 4,
        out_shape=[both] * 3 + [jax.ShapeDtypeStruct((2 * rows, cols), mine.dtype)],
        **params(12, 0.2),
    )(me.reshape(1), mine, other, *eigs)


def score_kernel(me, pick, grid, *refs):
    pieces, eig_own, in_own, packs = refs[:4], refs[4], refs[5], refs[6:9]
    out, rot, rot_t, ti_t = refs[9:]
    gather_rows(me, pieces, rot)
    width = eig_own.shape[0]
    eigs = [eig_own] + [p.at[:width, :] for p in packs]
    ins = [in_own] + [p.at[width:, :] for p in packs]
    for n in range(4):
        ti_t[n] = ins[n][256:, :].T
    for n in range(rot.shape[1] // 128):
        rot_t[n * 128 : (n + 1) * 128, :] = rot[:, n * 128 : (n + 1) * 128].T
    damp = [grid[pick[s]] for s in range(2)]
    weights = [None, None]
    for k in range(4):
        diag = eigs[k][...].astype(F32)
        for s in range(2):
            tokens = slice(s * 128, (s + 1) * 128)
            rotated = jnp.dot(rot_t[:, tokens], ins[k][tokens, :], preferred_element_type=F32)
            precond = (rotated / (diag + damp[s])).astype(BF)
            w = jnp.dot(precond, ti_t[k], preferred_element_type=F32)
            weights[s] = w if weights[s] is None else weights[s] + w
    train = rot_t[:, 256:].astype(F32)
    both = jnp.concatenate([jnp.sum(w * train, axis=0, keepdims=True) for w in weights], axis=0) * SCALE
    out[...] = jnp.broadcast_to(both[None], out.shape)


def score(me, pick, grid, pieces, eig, rot_in, packs):
    tokens, cols = pieces[0].shape
    return pl.pallas_call(
        score_kernel,
        in_specs=[SMEM] * 3 + [VMEM] * 9,
        out_specs=VMEM,
        out_shape=jax.ShapeDtypeStruct((16, 2, 256), F32),
        scratch_shapes=[
            pltpu.VMEM((4 * tokens, cols), BF),
            pltpu.VMEM((cols, 4 * tokens), BF),
            pltpu.VMEM((4, 256, 256), BF),
        ],
        **params(24, 3),
    )(me.reshape(1), pick, grid, *pieces, eig, rot_in, *packs)


def tie(value, *after):
    return lax.optimization_barrier((value, *after))[0]


def swap(value, axis, bit):
    size = 2 if axis in ("c", "zh") else 4
    return lax.ppermute(value, axis, [(i, i ^ bit) for i in range(size)])


def body(acts, out_grads, train_acts, train_grads, basis_in, basis_out, eig, grid, pick):
    y, x, c = lax.axis_index("y"), lax.axis_index("x"), lax.axis_index("c").astype(jnp.int32)
    first = jnp.where(c == 0, x, y).astype(jnp.int32)
    second = jnp.where(c == 0, y, x).astype(jnp.int32)
    width = basis_out.shape[1] // 4

    grads = (out_grads, train_grads)
    two_q, two_t, mine, other = open_mm(first, c, grads, basis_out, (acts, train_acts), basis_in, width)
    relay_q, relay_t = move(two_q, FIRST[1]), move(two_t, FIRST[3])
    in_chip = add(F32, mine, swap(other, "c", 1))
    up_q, up_t, down_q, down_t = lead_mm(*grads, basis_out, tie(first, two_q), (1, 3), width)
    from_down_t, from_up_q = move(up_t, FIRST[1]), move(down_q, FIRST[3])
    in_half = add(F32, in_chip, swap(in_chip, "zl", 1))
    up_q, down_t = add(BF, tie(up_q, in_chip), relay_q), add(BF, tie(down_t, in_chip), relay_t)
    from_down_q, from_up_t = move(up_q, FIRST[1]), move(down_t, FIRST[3])
    own_q, own_t = block_mm(*grads, basis_out, tie(first, up_q, down_t), (0,), width, (F32,))
    eig_own, *eig_send = pick_blocks(eig, tie(first, own_q), width)
    far_half = swap(add(BF, in_half), "zl", 2)

    *send, keep = sum_blocks(second, own_q, own_t, from_down_q, from_up_q, from_down_t, from_up_t)
    got = [move(v, SECOND[k]) for k, v in zip(HOPS, send)]
    in_half = add(BF, in_half, tie(far_half, send[0]))
    in_other = swap(in_half, "c", 1)
    *packs, rot_in = pack(c, in_half, in_other, eig_send)
    total = add(F32, tie(keep, rot_in), *got)
    near = add(BF, total)
    packs = [move(v, FIRST[k]) for k, v in zip(HOPS, packs)]
    total = tie(add(BF, total, swap(near, "zh", 1), us=4), packs[1])
    pieces = [total] + [move(total, SECOND[k]) for k in HOPS]
    part = score(second, pick, grid, pieces, eig_own, rot_in, packs)

    over = jnp.sum(lax.all_to_all(part, ("y", "x"), 0, 0, tiled=True), axis=0)
    over = jnp.broadcast_to(over[None], (16, *over.shape))
    return jnp.sum(lax.all_to_all(over, ("zh", "zl", "c"), 0, 0, tiled=True), axis=0)


def solution(mesh):
    fine = Mesh(mesh.devices.reshape(SIZES), ALL)
    aa, ga = ("y", "x", "zh"), ("zl", "c")
    return jax.shard_map(
        body,
        mesh=fine,
        in_specs=(
            P(None, ga),
            P(None, aa),
            P(None, ga),
            P(None, aa),
            P(ga, aa),
            P(aa, ga),
            P(ga, aa),
            P(),
            P(),
        ),
        out_specs=P(),
        check_vma=False,
    )
```

```python
import functools
import itertools
import math

import jax
import jax.numpy as jnp
from jax import lax
from jax.experimental import pallas as pl
from jax.experimental.pallas import tpu as pltpu
from jax.sharding import Mesh, PartitionSpec as P

D_IN = 8192
D_OUT = 28672
SIZES = (4, 4, 2, 4, 2)
ALL = ("y", "x", "zh", "zl", "c")
SCALE = 1.0 / math.sqrt(D_IN * D_OUT)
BF = jnp.bfloat16
F32 = jnp.float32
MIB = 1024 * 1024


def flat(place):
    n = 0
    for size, at in zip(SIZES, place):
        n = n * size + at
    return n


def shift(k, first):
    pairs = []
    for y, x, zh, zl, c in itertools.product(*(range(s) for s in SIZES)):
        if (c == 0) == first:
            to = (y, (x + k) % 4, zh, zl, c)
        else:
            to = ((y + k) % 4, x, zh, zl, c)
        pairs.append((flat((y, x, zh, zl, c)), flat(to)))
    return pairs


FIRST = {k: shift(k, True) for k in (1, 2, 3)}
SECOND = {k: shift(k, False) for k in (1, 2, 3)}
HOPS = (2, 1, 3)


def move(value, pairs):
    return lax.ppermute(value, ALL, pairs)


def params(mib, us):
    return {
        "compiler_params": pltpu.CompilerParams(vmem_limit_bytes=mib * MIB),
        "cost_estimate": pl.CostEstimate(flops=int(us * 1.15e9), bytes_accessed=0, transcendentals=0),
    }


SMEM = pl.BlockSpec(memory_space=pltpu.SMEM)
VMEM = pl.BlockSpec(memory_space=pltpu.VMEM)


def lead_kernel(hops, at, q_hbm, t_hbm, b_hbm, *refs):
    outs, (q, t, b, sems) = refs[: 2 * len(hops)], refs[2 * len(hops) :]
    width = outs[0].shape[1]
    loads = [pltpu.make_async_copy(q_hbm, q, sems.at[0]), pltpu.make_async_copy(t_hbm, t, sems.at[1])]
    for n, k in enumerate(hops):
        cols = pl.ds(pl.multiple_of(lax.rem(at[0] + k, 4) * width, width), width)
        loads.append(pltpu.make_async_copy(b_hbm.at[:, cols], b.at[n], sems.at[2 + n]))
    for n in (0, 2, 1, *range(3, len(loads))):
        loads[n].start()
    for n in range(len(hops)):
        loads[2 + n].wait()
        for m, rows in enumerate((q, t)):
            if n == 0:
                loads[m].wait()
            dst = outs[2 * n + m]
            dst[...] = jnp.dot(rows[...], b[n], preferred_element_type=F32).astype(dst.dtype)


def lead_mm(q, t, basis, me, hops, width):
    rows, depth = q.shape
    hbm = pl.BlockSpec(memory_space=pltpu.HBM)
    return pl.pallas_call(
        functools.partial(lead_kernel, hops),
        in_specs=[SMEM, hbm, hbm, hbm],
        out_specs=[VMEM] * (2 * len(hops)),
        out_shape=[jax.ShapeDtypeStruct((rows, width), BF)] * (2 * len(hops)),
        scratch_shapes=[
            pltpu.VMEM((rows, depth), BF),
            pltpu.VMEM((rows, depth), BF),
            pltpu.VMEM((len(hops), depth, width), BF),
            pltpu.SemaphoreType.DMA((2 + len(hops),)),
        ],
        **params(58, 5),
    )(me.reshape(1), q, t, basis)


def open_kernel(at, core_at, q_hbm, t_hbm, b_hbm, aq_hbm, at_hbm, bi_hbm, oq, ot, mine, other, q, t, b, aq, ta, bi, sems):
    width = oq.shape[1]
    cols = pl.ds(pl.multiple_of(lax.rem(at[0] + 2, 4) * width, width), width)
    pairs = ((aq_hbm, aq), (at_hbm, ta), (bi_hbm, bi), (q_hbm, q), (b_hbm.at[:, cols], b), (t_hbm, t))
    loads = [pltpu.make_async_copy(src, dst, sems.at[n]) for n, (src, dst) in enumerate(pairs)]
    for load in loads:
        load.start()
    for load in loads[:3]:
        load.wait()
    for core in range(2):

        @pl.when(core_at[0] == core)
        def _():
            mine[...] = jnp.dot((aq, ta)[core][...], bi[...], preferred_element_type=F32)
            other[...] = jnp.dot((ta, aq)[core][...], bi[...], preferred_element_type=F32)

    loads[3].wait()
    loads[4].wait()
    oq[...] = jnp.dot(q[...], b[...], preferred_element_type=F32).astype(oq.dtype)
    loads[5].wait()
    ot[...] = jnp.dot(t[...], b[...], preferred_element_type=F32).astype(ot.dtype)


def open_mm(first, core, grads, basis_out, acts, basis_in, width):
    (rows, depth), (in_depth, in_width) = grads[0].shape, basis_in.shape
    hbm = pl.BlockSpec(memory_space=pltpu.HBM)
    return pl.pallas_call(
        open_kernel,
        in_specs=[SMEM] * 2 + [hbm] * 6,
        out_specs=[VMEM] * 4,
        out_shape=[jax.ShapeDtypeStruct((rows, width), BF)] * 2 + [jax.ShapeDtypeStruct((rows, in_width), F32)] * 2,
        scratch_shapes=[
            pltpu.VMEM((rows, depth), BF),
            pltpu.VMEM((rows, depth), BF),
            pltpu.VMEM((depth, width), BF),
            pltpu.VMEM((rows, in_depth), BF),
            pltpu.VMEM((rows, in_depth), BF),
            pltpu.VMEM((in_depth, in_width), BF),
            pltpu.SemaphoreType.DMA((6,)),
        ],
        **params(58, 4.5),
    )(first.reshape(1), core.reshape(1), *grads, basis_out, *acts, basis_in)


def mm_kernel(hops, at, q_ref, t_ref, b_ref, *outs):
    width = outs[0].shape[1]
    blocks = b_ref.shape[1] // width
    for n, k in enumerate(hops):
        if blocks == 1:
            basis = b_ref[...]
        else:
            basis = b_ref[:, pl.ds(pl.multiple_of(lax.rem(at[0] + k, blocks) * width, width), width)]
        for ref, dst in ((q_ref, outs[2 * n]), (t_ref, outs[2 * n + 1])):
            dst[...] = jnp.dot(ref[...], basis, preferred_element_type=F32).astype(dst.dtype)


def block_mm(q, t, basis, me, hops, width, dtypes):
    return pl.pallas_call(
        functools.partial(mm_kernel, hops),
        in_specs=[SMEM, VMEM, VMEM, VMEM],
        out_specs=[VMEM] * (2 * len(hops)),
        out_shape=[jax.ShapeDtypeStruct((q.shape[0], width), d) for d in dtypes for _ in range(2)],
        **params(20, 4),
    )(me.reshape(1), q, t, basis)


def pick_kernel(at, *refs):
    half = len(refs) // 2
    for src, dst in zip(refs[:half], refs[half:]):
        dst[...] = src[...]


def pick_blocks(array, me, rows):
    cols = array.shape[1]
    return pl.pallas_call(
        pick_kernel,
        grid_spec=pltpu.PrefetchScalarGridSpec(
            num_scalar_prefetch=1,
            grid=(1,),
            in_specs=[
                pl.BlockSpec((rows, cols), lambda i, at, k=k: (lax.rem(at[0] + k, 4), 0)) for k in range(4)
            ],
            out_specs=[pl.BlockSpec((rows, cols), lambda i, at: (0, 0))] * 4,
        ),
        out_shape=[jax.ShapeDtypeStruct((rows, cols), array.dtype)] * 4,
        **params(16, 1.2),
    )(me.reshape(1), array, array, array, array)


def sum_kernel(at, own_q, own_t, q1, q2, t1, t2, o2, o1, o3, keep):
    part = keep.shape[0] // 2
    for hop, dst in ((2, o2), (1, o1), (3, o3), (0, keep)):
        rows = pl.ds(pl.multiple_of(lax.rem(at[0] + hop, 4) * part, part), part)
        for n, (a, b, c) in enumerate(((own_q, q1, q2), (own_t, t1, t2))):
            total = a[rows, :] + b[rows, :].astype(F32) + c[rows, :].astype(F32)
            dst[n * part : (n + 1) * part, :] = total.astype(dst.dtype)


def sum_blocks(me, *parts):
    rows, cols = parts[0].shape
    small = jax.ShapeDtypeStruct((rows // 2, cols), BF)
    return pl.pallas_call(
        sum_kernel,
        in_specs=[SMEM] + [VMEM] * 6,
        out_specs=[VMEM] * 4,
        out_shape=[small, small, small, jax.ShapeDtypeStruct((rows // 2, cols), F32)],
        **params(12, 1.6),
    )(me.reshape(1), *parts)


def gather_rows(me, pieces, whole):
    part = pieces[0].shape[0] // 2
    for k, piece in zip((0, *HOPS), pieces):
        row = lax.rem(me[0] + 4 - k, 4) * part
        whole[pl.ds(pl.multiple_of(row, part), part), :] = piece[:part, :]
        whole[pl.ds(pl.multiple_of(row + 4 * part, part), part), :] = piece[part:, :]


def add_kernel(*refs):
    *parts, out = refs
    total = parts[0][...].astype(F32)
    for part in parts[1:]:
        total = total + part[...].astype(F32)
    out[...] = total.astype(out.dtype)


def add(dtype, *parts, us=0.1):
    return pl.pallas_call(
        add_kernel,
        in_specs=[VMEM] * len(parts),
        out_specs=VMEM,
        out_shape=jax.ShapeDtypeStruct(parts[0].shape, dtype),
        **params(8, us),
    )(*parts)


def pack_kernel(at, mine, other, e1, e2, e3, up, down, rot_in):
    part = mine.shape[0]
    rot_in[pl.ds(pl.multiple_of(at[0] * part, part), part), :] = mine[...]
    rot_in[pl.ds(pl.multiple_of((1 - at[0]) * part, part), part), :] = other[...]
    rows = e1.shape[0]
    half = rows // 2
    for n, (eig, dst) in enumerate(((e1, up), (e3, down))):
        dst[:rows, :] = eig[...]
        dst[rows : rows + part, :] = rot_in[(1 - n) * part : (2 - n) * part, :]
        dst[rows + part : rows + 2 * part, :] = rot_in[n * part : (n + 1) * part, :]
        dst[rows + 2 * part :, :] = e2[n * half : (n + 1) * half, :]


def pack(me, mine, other, e1, e2, e3):
    rows, cols = mine.shape
    both = jax.ShapeDtypeStruct((e1.shape[0] * 3 // 2 + 2 * rows, cols), mine.dtype)
    return pl.pallas_call(
        pack_kernel,
        in_specs=[SMEM] + [VMEM] * 5,
        out_specs=[VMEM] * 3,
        out_shape=[both] * 2 + [jax.ShapeDtypeStruct((2 * rows, cols), mine.dtype)],
        **params(12, 0.2),
    )(me.reshape(1), mine, other, e1, e2, e3)


def onward_kernel(low, high, up, down):
    rows = up.shape[0]
    up[...] = low[low.shape[0] - rows :, :]
    down[...] = high[high.shape[0] - rows :, :]


def onward(low, high, rows):
    out = jax.ShapeDtypeStruct((rows, low.shape[1]), low.dtype)
    return pl.pallas_call(
        onward_kernel,
        in_specs=[VMEM] * 2,
        out_specs=[VMEM] * 2,
        out_shape=[out] * 2,
        **params(8, 0.1),
    )(low, high)


def score_kernel(me, pick, grid, *refs):
    pieces, eig_own, in_own, low, high, far_low, far_high = refs[:4], *refs[4:10]
    out, rot, rot_t, ti_t, eig_far, in_near = refs[10:]
    gather_rows(me, pieces, rot)
    width = eig_own.shape[0]
    part = in_own.shape[0] // 2
    in_near[0, :part, :] = low[width + part : width + 2 * part, :]
    in_near[0, part:, :] = low[width : width + part, :]
    in_near[1, :part, :] = far_low[:part, :]
    in_near[1, part:, :] = far_high[:part, :]
    eig_far[: width // 2, :] = far_low[part:, :]
    eig_far[width // 2 :, :] = far_high[part:, :]
    eigs = [eig_own, low.at[:width, :], high.at[:width, :], eig_far]
    ins = [in_own, in_near.at[0], high.at[width : width + 2 * part, :], in_near.at[1]]
    for n in range(4):
        ti_t[n] = ins[n][256:, :].T
    for n in range(rot.shape[1] // 128):
        rot_t[n * 128 : (n + 1) * 128, :] = rot[:, n * 128 : (n + 1) * 128].T
    damp = [grid[pick[s]] for s in range(2)]
    weights = [None, None]
    for k in range(4):
        diag = eigs[k][...].astype(F32)
        for s in range(2):
            tokens = slice(s * 128, (s + 1) * 128)
            rotated = jnp.dot(rot_t[:, tokens], ins[k][tokens, :], preferred_element_type=F32)
            precond = (rotated / (diag + damp[s])).astype(BF)
            w = jnp.dot(precond, ti_t[k], preferred_element_type=F32)
            weights[s] = w if weights[s] is None else weights[s] + w
    train = rot_t[:, 256:].astype(F32)
    both = jnp.concatenate([jnp.sum(w * train, axis=0, keepdims=True) for w in weights], axis=0) * SCALE
    out[...] = jnp.broadcast_to(both[None], out.shape)


def score(me, pick, grid, pieces, eig, rot_in, messages):
    tokens, cols = pieces[0].shape
    return pl.pallas_call(
        score_kernel,
        in_specs=[SMEM] * 3 + [VMEM] * 10,
        out_specs=VMEM,
        out_shape=jax.ShapeDtypeStruct((16, 2, 256), F32),
        scratch_shapes=[
            pltpu.VMEM((4 * tokens, cols), BF),
            pltpu.VMEM((cols, 4 * tokens), BF),
            pltpu.VMEM((4, 256, 256), BF),
            pltpu.VMEM(eig.shape, BF),
            pltpu.VMEM((2, *rot_in.shape), BF),
        ],
        **params(24, 3),
    )(me.reshape(1), pick, grid, *pieces, eig, rot_in, *messages)


def tie(value, *after):
    return lax.optimization_barrier((value, *after))[0]


def swap(value, axis, bit):
    size = 2 if axis in ("c", "zh") else 4
    return lax.ppermute(value, axis, [(i, i ^ bit) for i in range(size)])


def body(acts, out_grads, train_acts, train_grads, basis_in, basis_out, eig, grid, pick):
    y, x, c = lax.axis_index("y"), lax.axis_index("x"), lax.axis_index("c").astype(jnp.int32)
    first = jnp.where(c == 0, x, y).astype(jnp.int32)
    second = jnp.where(c == 0, y, x).astype(jnp.int32)
    width = basis_out.shape[1] // 4

    grads = (out_grads, train_grads)
    two_q, two_t, mine, other = open_mm(first, c, grads, basis_out, (acts, train_acts), basis_in, width)
    relay_q, relay_t = move(two_q, FIRST[1]), move(two_t, FIRST[3])
    in_chip = add(F32, mine, swap(other, "c", 1))
    up_q, up_t, down_q, down_t = lead_mm(*grads, basis_out, tie(first, two_q), (1, 3), width)
    from_down_t, from_up_q = move(up_t, FIRST[1]), move(down_q, FIRST[3])
    in_half = add(F32, in_chip, swap(in_chip, "zl", 1))
    up_q, down_t = add(BF, tie(up_q, in_chip), relay_q), add(BF, tie(down_t, in_chip), relay_t)
    from_down_q, from_up_t = move(up_q, FIRST[1]), move(down_t, FIRST[3])
    own_q, own_t = block_mm(*grads, basis_out, tie(first, up_q, down_t), (0,), width, (F32,))
    eig_own, *eig_send = pick_blocks(eig, tie(first, own_q), width)
    far_half = swap(add(BF, in_half, us=0.1), "zl", 2)

    *send, keep = sum_blocks(second, own_q, own_t, from_down_q, from_up_q, from_down_t, from_up_t)
    got = [move(v, SECOND[k]) for k, v in zip(HOPS, send)]
    in_half = add(BF, in_half, tie(far_half, send[0]))
    in_other = swap(in_half, "c", 1)
    up, down, rot_in = pack(c, in_half, in_other, *eig_send)
    total = add(F32, tie(keep, rot_in), *got, us=8)
    near = add(BF, total)
    low, high = move(up, FIRST[1]), move(down, FIRST[3])
    up, down = onward(low, high, width // 2 + in_half.shape[0])
    messages = low, high, move(up, FIRST[1]), move(down, FIRST[3])
    total = add(BF, total, swap(near, "zh", 1), us=4)
    pieces = [total] + [move(total, SECOND[k]) for k in HOPS]
    part = score(second, pick, grid, pieces, eig_own, rot_in, messages)

    over = jnp.sum(lax.all_to_all(part, ("zh", "zl", "c"), 0, 0, tiled=True), axis=0)
    over = jnp.broadcast_to(over[None], (16, *over.shape))
    return jnp.sum(lax.all_to_all(over, ("y", "x"), 0, 0, tiled=True), axis=0)


def solution(mesh):
    fine = Mesh(mesh.devices.reshape(SIZES), ALL)
    aa, ga = ("y", "x", "zh"), ("zl", "c")
    return jax.shard_map(
        body,
        mesh=fine,
        in_specs=(
            P(None, ga),
            P(None, aa),
            P(None, ga),
            P(None, aa),
            P(ga, aa),
            P(aa, ga),
            P(ga, aa),
            P(),
            P(),
        ),
        out_specs=P(),
        check_vma=False,
    )
```

```python
import functools
import itertools
import math

import jax
import jax.numpy as jnp
from jax import lax
from jax.experimental import pallas as pl
from jax.experimental.pallas import tpu as pltpu
from jax.sharding import Mesh, PartitionSpec as P

D_IN = 8192
D_OUT = 28672
SIZES = (4, 4, 2, 4, 2)
ALL = ("y", "x", "zh", "zl", "c")
SCALE = 1.0 / math.sqrt(D_IN * D_OUT)
BF = jnp.bfloat16
F32 = jnp.float32
MIB = 1024 * 1024


def flat(place):
    n = 0
    for size, at in zip(SIZES, place):
        n = n * size + at
    return n


def shift(k, first):
    pairs = []
    for y, x, zh, zl, c in itertools.product(*(range(s) for s in SIZES)):
        if (c == 0) == first:
            to = (y, (x + k) % 4, zh, zl, c)
        else:
            to = ((y + k) % 4, x, zh, zl, c)
        pairs.append((flat((y, x, zh, zl, c)), flat(to)))
    return pairs


FIRST = {k: shift(k, True) for k in (1, 2, 3)}
SECOND = {k: shift(k, False) for k in (1, 2, 3)}
HOPS = (2, 1, 3)


def move(value, pairs):
    return lax.ppermute(value, ALL, pairs)


def params(mib, us):
    return {
        "compiler_params": pltpu.CompilerParams(vmem_limit_bytes=mib * MIB),
        "cost_estimate": pl.CostEstimate(flops=int(us * 1.15e9), bytes_accessed=0, transcendentals=0),
    }


SMEM = pl.BlockSpec(memory_space=pltpu.SMEM)
VMEM = pl.BlockSpec(memory_space=pltpu.VMEM)


def lead_kernel(hops, at, q_hbm, t_hbm, b_hbm, *refs):
    outs, (q, t, b, sems) = refs[: 2 * len(hops)], refs[2 * len(hops) :]
    width = outs[0].shape[1]
    loads = [pltpu.make_async_copy(q_hbm, q, sems.at[0]), pltpu.make_async_copy(t_hbm, t, sems.at[1])]
    for n, k in enumerate(hops):
        cols = pl.ds(pl.multiple_of(lax.rem(at[0] + k, 4) * width, width), width)
        loads.append(pltpu.make_async_copy(b_hbm.at[:, cols], b.at[n], sems.at[2 + n]))
    for n in (0, 2, 1, *range(3, len(loads))):
        loads[n].start()
    for n in range(len(hops)):
        loads[2 + n].wait()
        for m, rows in enumerate((q, t)):
            if n == 0:
                loads[m].wait()
            dst = outs[2 * n + m]
            dst[...] = jnp.dot(rows[...], b[n], preferred_element_type=F32).astype(dst.dtype)


def lead_mm(q, t, basis, me, hops, width):
    rows, depth = q.shape
    hbm = pl.BlockSpec(memory_space=pltpu.HBM)
    return pl.pallas_call(
        functools.partial(lead_kernel, hops),
        in_specs=[SMEM, hbm, hbm, hbm],
        out_specs=[VMEM] * (2 * len(hops)),
        out_shape=[jax.ShapeDtypeStruct((rows, width), BF)] * (2 * len(hops)),
        scratch_shapes=[
            pltpu.VMEM((rows, depth), BF),
            pltpu.VMEM((rows, depth), BF),
            pltpu.VMEM((len(hops), depth, width), BF),
            pltpu.SemaphoreType.DMA((2 + len(hops),)),
        ],
        **params(58, 5),
    )(me.reshape(1), q, t, basis)


def open_kernel(at, core_at, q_hbm, t_hbm, b_hbm, aq_hbm, at_hbm, bi_hbm, oq, ot, mine, other, q, t, b, aq, ta, bi, sems):
    width = oq.shape[1]
    cols = pl.ds(pl.multiple_of(lax.rem(at[0] + 2, 4) * width, width), width)
    pairs = ((aq_hbm, aq), (at_hbm, ta), (bi_hbm, bi), (q_hbm, q), (b_hbm.at[:, cols], b), (t_hbm, t))
    loads = [pltpu.make_async_copy(src, dst, sems.at[n]) for n, (src, dst) in enumerate(pairs)]
    for load in loads:
        load.start()
    for load in loads[:3]:
        load.wait()
    for core in range(2):

        @pl.when(core_at[0] == core)
        def _():
            mine[...] = jnp.dot((aq, ta)[core][...], bi[...], preferred_element_type=F32)
            other[...] = jnp.dot((ta, aq)[core][...], bi[...], preferred_element_type=F32)

    loads[3].wait()
    loads[4].wait()
    oq[...] = jnp.dot(q[...], b[...], preferred_element_type=F32).astype(oq.dtype)
    loads[5].wait()
    ot[...] = jnp.dot(t[...], b[...], preferred_element_type=F32).astype(ot.dtype)


def open_mm(first, core, grads, basis_out, acts, basis_in, width):
    (rows, depth), (in_depth, in_width) = grads[0].shape, basis_in.shape
    hbm = pl.BlockSpec(memory_space=pltpu.HBM)
    return pl.pallas_call(
        open_kernel,
        in_specs=[SMEM] * 2 + [hbm] * 6,
        out_specs=[VMEM] * 4,
        out_shape=[jax.ShapeDtypeStruct((rows, width), BF)] * 2 + [jax.ShapeDtypeStruct((rows, in_width), F32)] * 2,
        scratch_shapes=[
            pltpu.VMEM((rows, depth), BF),
            pltpu.VMEM((rows, depth), BF),
            pltpu.VMEM((depth, width), BF),
            pltpu.VMEM((rows, in_depth), BF),
            pltpu.VMEM((rows, in_depth), BF),
            pltpu.VMEM((in_depth, in_width), BF),
            pltpu.SemaphoreType.DMA((6,)),
        ],
        **params(58, 4.5),
    )(first.reshape(1), core.reshape(1), *grads, basis_out, *acts, basis_in)


def mm_kernel(hops, at, q_ref, t_ref, b_ref, *outs):
    width = outs[0].shape[1]
    blocks = b_ref.shape[1] // width
    for n, k in enumerate(hops):
        if blocks == 1:
            basis = b_ref[...]
        else:
            basis = b_ref[:, pl.ds(pl.multiple_of(lax.rem(at[0] + k, blocks) * width, width), width)]
        for ref, dst in ((q_ref, outs[2 * n]), (t_ref, outs[2 * n + 1])):
            dst[...] = jnp.dot(ref[...], basis, preferred_element_type=F32).astype(dst.dtype)


def block_mm(q, t, basis, me, hops, width, dtypes):
    return pl.pallas_call(
        functools.partial(mm_kernel, hops),
        in_specs=[SMEM, VMEM, VMEM, VMEM],
        out_specs=[VMEM] * (2 * len(hops)),
        out_shape=[jax.ShapeDtypeStruct((q.shape[0], width), d) for d in dtypes for _ in range(2)],
        **params(20, 4),
    )(me.reshape(1), q, t, basis)


def pick_kernel(at, *refs):
    half = len(refs) // 2
    for src, dst in zip(refs[:half], refs[half:]):
        dst[...] = src[...]


def pick_blocks(array, me, rows):
    cols = array.shape[1]
    return pl.pallas_call(
        pick_kernel,
        grid_spec=pltpu.PrefetchScalarGridSpec(
            num_scalar_prefetch=1,
            grid=(1,),
            in_specs=[
                pl.BlockSpec((rows, cols), lambda i, at, k=k: (lax.rem(at[0] + k, 4), 0)) for k in range(4)
            ],
            out_specs=[pl.BlockSpec((rows, cols), lambda i, at: (0, 0))] * 4,
        ),
        out_shape=[jax.ShapeDtypeStruct((rows, cols), array.dtype)] * 4,
        **params(16, 1.2),
    )(me.reshape(1), array, array, array, array)


def sum_kernel(at, own_q, own_t, q1, q2, t1, t2, o2, o1, o3, keep):
    part = keep.shape[0] // 2
    for hop, dst in ((2, o2), (1, o1), (3, o3), (0, keep)):
        rows = pl.ds(pl.multiple_of(lax.rem(at[0] + hop, 4) * part, part), part)
        for n, (a, b, c) in enumerate(((own_q, q1, q2), (own_t, t1, t2))):
            total = a[rows, :] + b[rows, :].astype(F32) + c[rows, :].astype(F32)
            dst[n * part : (n + 1) * part, :] = total.astype(dst.dtype)


def sum_blocks(me, *parts):
    rows, cols = parts[0].shape
    small = jax.ShapeDtypeStruct((rows // 2, cols), BF)
    return pl.pallas_call(
        sum_kernel,
        in_specs=[SMEM] + [VMEM] * 6,
        out_specs=[VMEM] * 4,
        out_shape=[small, small, small, jax.ShapeDtypeStruct((rows // 2, cols), F32)],
        **params(12, 1.6),
    )(me.reshape(1), *parts)


def gather_rows(me, pieces, whole):
    part = pieces[0].shape[0] // 2
    for k, piece in zip((0, *HOPS), pieces):
        row = lax.rem(me[0] + 4 - k, 4) * part
        whole[pl.ds(pl.multiple_of(row, part), part), :] = piece[:part, :]
        whole[pl.ds(pl.multiple_of(row + 4 * part, part), part), :] = piece[part:, :]


def add_kernel(*refs):
    *parts, out = refs
    total = parts[0][...].astype(F32)
    for part in parts[1:]:
        total = total + part[...].astype(F32)
    out[...] = total.astype(out.dtype)


def add(dtype, *parts, us=0.1):
    return pl.pallas_call(
        add_kernel,
        in_specs=[VMEM] * len(parts),
        out_specs=VMEM,
        out_shape=jax.ShapeDtypeStruct(parts[0].shape, dtype),
        **params(8, us),
    )(*parts)


def pack_kernel(e1, e2, e3, up, down):
    rows = e1.shape[0]
    half = rows // 2
    for n, (eig, dst) in enumerate(((e1, up), (e3, down))):
        dst[:rows, :] = eig[...]
        dst[rows:, :] = e2[n * half : (n + 1) * half, :]


def pack(e1, e2, e3):
    rows, cols = e1.shape
    return pl.pallas_call(
        pack_kernel,
        in_specs=[VMEM] * 3,
        out_specs=[VMEM] * 2,
        out_shape=[jax.ShapeDtypeStruct((rows * 3 // 2, cols), e1.dtype)] * 2,
        **params(12, 0.2),
    )(e1, e2, e3)


def join_kernel(at, mine, other, whole):
    part = mine.shape[0]
    whole[pl.ds(pl.multiple_of(at[0] * part, part), part), :] = mine[...]
    whole[pl.ds(pl.multiple_of((1 - at[0]) * part, part), part), :] = other[...]


def join(me, mine, other):
    return pl.pallas_call(
        join_kernel,
        in_specs=[SMEM, VMEM, VMEM],
        out_specs=VMEM,
        out_shape=jax.ShapeDtypeStruct((2 * mine.shape[0], mine.shape[1]), mine.dtype),
        **params(8, 0.1),
    )(me.reshape(1), mine, other)


def onward_kernel(low, in_low, high, in_high, up, down):
    part = in_low.shape[0] // 2
    half = up.shape[0] - part
    for n, (eig, rot_in, dst) in enumerate(((low, in_low, up), (high, in_high, down))):
        dst[:part, :] = rot_in[n * part : (n + 1) * part, :]
        dst[part:, :] = eig[2 * half :, :]


def onward(low, in_low, high, in_high):
    out = jax.ShapeDtypeStruct((low.shape[0] // 3 + in_low.shape[0] // 2, low.shape[1]), low.dtype)
    return pl.pallas_call(
        onward_kernel,
        in_specs=[VMEM] * 4,
        out_specs=[VMEM] * 2,
        out_shape=[out] * 2,
        **params(8, 0.1),
    )(low, in_low, high, in_high)


def score_kernel(me, pick, grid, *refs):
    pieces, eig_own, in_own, low, in_low, high, in_high, far_low, far_high = refs[:4], *refs[4:12]
    out, rot, rot_t, ti_t, eig_far, in_far = refs[12:]
    gather_rows(me, pieces, rot)
    width = eig_own.shape[0]
    part = in_own.shape[0] // 2
    in_far[:part, :] = far_low[:part, :]
    in_far[part:, :] = far_high[:part, :]
    eig_far[: width // 2, :] = far_low[part:, :]
    eig_far[width // 2 :, :] = far_high[part:, :]
    eigs = [eig_own, low.at[:width, :], high.at[:width, :], eig_far]
    ins = [in_own, in_low, in_high, in_far]
    for n in range(4):
        ti_t[n] = ins[n][256:, :].T
    for n in range(rot.shape[1] // 128):
        rot_t[n * 128 : (n + 1) * 128, :] = rot[:, n * 128 : (n + 1) * 128].T
    damp = [grid[pick[s]] for s in range(2)]
    weights = [None, None]
    for k in range(4):
        diag = eigs[k][...].astype(F32)
        for s in range(2):
            tokens = slice(s * 128, (s + 1) * 128)
            rotated = jnp.dot(rot_t[:, tokens], ins[k][tokens, :], preferred_element_type=F32)
            precond = (rotated / (diag + damp[s])).astype(BF)
            w = jnp.dot(precond, ti_t[k], preferred_element_type=F32)
            weights[s] = w if weights[s] is None else weights[s] + w
    train = rot_t[:, 256:].astype(F32)
    both = jnp.concatenate([jnp.sum(w * train, axis=0, keepdims=True) for w in weights], axis=0) * SCALE
    out[...] = jnp.broadcast_to(both[None], out.shape)


def score(me, pick, grid, pieces, eig, rot_in, messages):
    tokens, cols = pieces[0].shape
    return pl.pallas_call(
        score_kernel,
        in_specs=[SMEM] * 3 + [VMEM] * 12,
        out_specs=VMEM,
        out_shape=jax.ShapeDtypeStruct((16, 2, 256), F32),
        scratch_shapes=[
            pltpu.VMEM((4 * tokens, cols), BF),
            pltpu.VMEM((cols, 4 * tokens), BF),
            pltpu.VMEM((4, 256, 256), BF),
            pltpu.VMEM(eig.shape, BF),
            pltpu.VMEM(rot_in.shape, BF),
        ],
        **params(24, 3),
    )(me.reshape(1), pick, grid, *pieces, eig, rot_in, *messages)


def tie(value, *after):
    return lax.optimization_barrier((value, *after))[0]


def swap(value, axis, bit):
    size = 2 if axis in ("c", "zh") else 4
    return lax.ppermute(value, axis, [(i, i ^ bit) for i in range(size)])


def body(acts, out_grads, train_acts, train_grads, basis_in, basis_out, eig, grid, pick):
    y, x, c = lax.axis_index("y"), lax.axis_index("x"), lax.axis_index("c").astype(jnp.int32)
    first = jnp.where(c == 0, x, y).astype(jnp.int32)
    second = jnp.where(c == 0, y, x).astype(jnp.int32)
    width = basis_out.shape[1] // 4

    grads = (out_grads, train_grads)
    two_q, two_t, mine, other = open_mm(first, c, grads, basis_out, (acts, train_acts), basis_in, width)
    relay_q, relay_t = move(two_q, FIRST[1]), move(two_t, FIRST[3])
    in_chip = add(F32, mine, swap(other, "c", 1))
    up_q, up_t, down_q, down_t = lead_mm(*grads, basis_out, tie(first, two_q), (1, 3), width)
    from_down_t, from_up_q = move(up_t, FIRST[1]), move(down_q, FIRST[3])
    in_half = add(F32, in_chip, swap(in_chip, "zl", 1))
    up_q, down_t = add(BF, up_q, relay_q), add(BF, down_t, relay_t)
    from_down_q, from_up_t = move(up_q, FIRST[1]), move(down_t, FIRST[3])
    eig_own, *eigs = pick_blocks(eig, tie(first, up_q), width)
    up, down = pack(*eigs)
    low = move(tie(up, from_down_t, from_up_q), FIRST[1])
    high = move(tie(down, from_down_t, from_up_q), FIRST[3])
    own_q, own_t = block_mm(*grads, basis_out, tie(first, up_q, down_t), (0,), width, (F32,))
    far_half = swap(add(BF, in_half), "zl", 2)

    *send, keep = sum_blocks(second, own_q, own_t, from_down_q, from_up_q, from_down_t, from_up_t)
    got = [move(v, SECOND[k]) for k, v in zip(HOPS, send)]
    in_half = add(BF, in_half, tie(far_half, send[0]))
    rot_in = join(c, in_half, swap(in_half, "c", 1))
    in_low, in_high = move(rot_in, FIRST[1]), move(rot_in, FIRST[3])
    total = add(F32, tie(keep, rot_in), *got, us=8)
    near = add(BF, total)
    up, down = onward(low, in_low, high, in_high)
    messages = low, in_low, high, in_high, move(up, FIRST[1]), move(down, FIRST[3])
    total = add(BF, total, swap(near, "zh", 1), us=4)
    pieces = [total] + [move(total, SECOND[k]) for k in HOPS]
    part = score(second, pick, grid, pieces, eig_own, rot_in, messages)

    over = jnp.sum(lax.all_to_all(part, ("zh", "zl", "c"), 0, 0, tiled=True), axis=0)
    over = jnp.broadcast_to(over[None], (16, *over.shape))
    return jnp.sum(lax.all_to_all(over, ("y", "x"), 0, 0, tiled=True), axis=0)


def solution(mesh):
    fine = Mesh(mesh.devices.reshape(SIZES), ALL)
    aa, ga = ("y", "x", "zh"), ("zl", "c")
    return jax.shard_map(
        body,
        mesh=fine,
        in_specs=(
            P(None, ga),
            P(None, aa),
            P(None, ga),
            P(None, aa),
            P(ga, aa),
            P(aa, ga),
            P(ga, aa),
            P(),
            P(),
        ),
        out_specs=P(),
        check_vma=False,
    )
```

```python
import functools
import itertools
import math

import jax
import jax.numpy as jnp
from jax import lax
from jax.experimental import pallas as pl
from jax.experimental.pallas import tpu as pltpu
from jax.sharding import Mesh, PartitionSpec as P

D_IN = 8192
D_OUT = 28672
SIZES = (4, 4, 2, 4, 2)
ALL = ("y", "x", "zh", "zl", "c")
SCALE = 1.0 / math.sqrt(D_IN * D_OUT)
BF = jnp.bfloat16
F32 = jnp.float32
MIB = 1024 * 1024


def flat(place):
    n = 0
    for size, at in zip(SIZES, place):
        n = n * size + at
    return n


def shift(k, first):
    pairs = []
    for y, x, zh, zl, c in itertools.product(*(range(s) for s in SIZES)):
        if (c == 0) == first:
            to = (y, (x + k) % 4, zh, zl, c)
        else:
            to = ((y + k) % 4, x, zh, zl, c)
        pairs.append((flat((y, x, zh, zl, c)), flat(to)))
    return pairs


FIRST = {k: shift(k, True) for k in (1, 2, 3)}
SECOND = {k: shift(k, False) for k in (1, 2, 3)}
HOPS = (2, 1, 3)


def move(value, pairs):
    return lax.ppermute(value, ALL, pairs)


def params(mib, us):
    return {
        "compiler_params": pltpu.CompilerParams(vmem_limit_bytes=mib * MIB),
        "cost_estimate": pl.CostEstimate(flops=int(us * 1.15e9), bytes_accessed=0, transcendentals=0),
    }


SMEM = pl.BlockSpec(memory_space=pltpu.SMEM)
VMEM = pl.BlockSpec(memory_space=pltpu.VMEM)


def lead_kernel(hops, at, q_hbm, t_hbm, b_hbm, *refs):
    outs, (q, t, b, sems) = refs[: 2 * len(hops)], refs[2 * len(hops) :]
    width = outs[0].shape[1]
    loads = [pltpu.make_async_copy(q_hbm, q, sems.at[0]), pltpu.make_async_copy(t_hbm, t, sems.at[1])]
    for n, k in enumerate(hops):
        cols = pl.ds(pl.multiple_of(lax.rem(at[0] + k, 4) * width, width), width)
        loads.append(pltpu.make_async_copy(b_hbm.at[:, cols], b.at[n], sems.at[2 + n]))
    for n in (0, 2, 1, *range(3, len(loads))):
        loads[n].start()
    for n in range(len(hops)):
        loads[2 + n].wait()
        for m, rows in enumerate((q, t)):
            if n == 0:
                loads[m].wait()
            dst = outs[2 * n + m]
            dst[...] = jnp.dot(rows[...], b[n], preferred_element_type=F32).astype(dst.dtype)


def lead_mm(q, t, basis, me, hops, width):
    rows, depth = q.shape
    hbm = pl.BlockSpec(memory_space=pltpu.HBM)
    return pl.pallas_call(
        functools.partial(lead_kernel, hops),
        in_specs=[SMEM, hbm, hbm, hbm],
        out_specs=[VMEM] * (2 * len(hops)),
        out_shape=[jax.ShapeDtypeStruct((rows, width), BF)] * (2 * len(hops)),
        scratch_shapes=[
            pltpu.VMEM((rows, depth), BF),
            pltpu.VMEM((rows, depth), BF),
            pltpu.VMEM((len(hops), depth, width), BF),
            pltpu.SemaphoreType.DMA((2 + len(hops),)),
        ],
        **params(58, 5),
    )(me.reshape(1), q, t, basis)


def open_kernel(at, core_at, q_hbm, t_hbm, b_hbm, aq_hbm, at_hbm, bi_hbm, oq, ot, mine, other, q, t, b, aq, ta, bi, sems):
    width = oq.shape[1]
    cols = pl.ds(pl.multiple_of(lax.rem(at[0] + 2, 4) * width, width), width)
    pairs = ((aq_hbm, aq), (at_hbm, ta), (bi_hbm, bi), (q_hbm, q), (b_hbm.at[:, cols], b), (t_hbm, t))
    loads = [pltpu.make_async_copy(src, dst, sems.at[n]) for n, (src, dst) in enumerate(pairs)]
    for load in loads:
        load.start()
    for load in loads[:3]:
        load.wait()
    for core in range(2):

        @pl.when(core_at[0] == core)
        def _():
            mine[...] = jnp.dot((aq, ta)[core][...], bi[...], preferred_element_type=F32)
            other[...] = jnp.dot((ta, aq)[core][...], bi[...], preferred_element_type=F32)

    loads[3].wait()
    loads[4].wait()
    oq[...] = jnp.dot(q[...], b[...], preferred_element_type=F32).astype(oq.dtype)
    loads[5].wait()
    ot[...] = jnp.dot(t[...], b[...], preferred_element_type=F32).astype(ot.dtype)


def open_mm(first, core, grads, basis_out, acts, basis_in, width):
    (rows, depth), (in_depth, in_width) = grads[0].shape, basis_in.shape
    hbm = pl.BlockSpec(memory_space=pltpu.HBM)
    return pl.pallas_call(
        open_kernel,
        in_specs=[SMEM] * 2 + [hbm] * 6,
        out_specs=[VMEM] * 4,
        out_shape=[jax.ShapeDtypeStruct((rows, width), BF)] * 2 + [jax.ShapeDtypeStruct((rows, in_width), F32)] * 2,
        scratch_shapes=[
            pltpu.VMEM((rows, depth), BF),
            pltpu.VMEM((rows, depth), BF),
            pltpu.VMEM((depth, width), BF),
            pltpu.VMEM((rows, in_depth), BF),
            pltpu.VMEM((rows, in_depth), BF),
            pltpu.VMEM((in_depth, in_width), BF),
            pltpu.SemaphoreType.DMA((6,)),
        ],
        **params(58, 4.5),
    )(first.reshape(1), core.reshape(1), *grads, basis_out, *acts, basis_in)


def mm_kernel(hops, at, q_ref, t_ref, b_ref, *outs):
    width = outs[0].shape[1]
    blocks = b_ref.shape[1] // width
    for n, k in enumerate(hops):
        if blocks == 1:
            basis = b_ref[...]
        else:
            basis = b_ref[:, pl.ds(pl.multiple_of(lax.rem(at[0] + k, blocks) * width, width), width)]
        for ref, dst in ((q_ref, outs[2 * n]), (t_ref, outs[2 * n + 1])):
            dst[...] = jnp.dot(ref[...], basis, preferred_element_type=F32).astype(dst.dtype)


def block_mm(q, t, basis, me, hops, width, dtypes):
    return pl.pallas_call(
        functools.partial(mm_kernel, hops),
        in_specs=[SMEM, VMEM, VMEM, VMEM],
        out_specs=[VMEM] * (2 * len(hops)),
        out_shape=[jax.ShapeDtypeStruct((q.shape[0], width), d) for d in dtypes for _ in range(2)],
        **params(20, 4),
    )(me.reshape(1), q, t, basis)


def pick_kernel(at, *refs):
    half = len(refs) // 2
    for src, dst in zip(refs[:half], refs[half:]):
        dst[...] = src[...]


def pick_blocks(array, me, rows):
    cols = array.shape[1]
    return pl.pallas_call(
        pick_kernel,
        grid_spec=pltpu.PrefetchScalarGridSpec(
            num_scalar_prefetch=1,
            grid=(1,),
            in_specs=[
                pl.BlockSpec((rows, cols), lambda i, at, k=k: (lax.rem(at[0] + k, 4), 0)) for k in range(4)
            ],
            out_specs=[pl.BlockSpec((rows, cols), lambda i, at: (0, 0))] * 4,
        ),
        out_shape=[jax.ShapeDtypeStruct((rows, cols), array.dtype)] * 4,
        **params(16, 1.2),
    )(me.reshape(1), array, array, array, array)


def sum_kernel(at, own_q, own_t, q1, q2, t1, t2, o2, o1, o3, keep):
    part = keep.shape[0] // 2
    for hop, dst in ((2, o2), (1, o1), (3, o3), (0, keep)):
        rows = pl.ds(pl.multiple_of(lax.rem(at[0] + hop, 4) * part, part), part)
        for n, (a, b, c) in enumerate(((own_q, q1, q2), (own_t, t1, t2))):
            total = a[rows, :] + b[rows, :].astype(F32) + c[rows, :].astype(F32)
            dst[n * part : (n + 1) * part, :] = total.astype(dst.dtype)


def sum_blocks(me, *parts):
    rows, cols = parts[0].shape
    small = jax.ShapeDtypeStruct((rows // 2, cols), BF)
    return pl.pallas_call(
        sum_kernel,
        in_specs=[SMEM] + [VMEM] * 6,
        out_specs=[VMEM] * 4,
        out_shape=[small, small, small, jax.ShapeDtypeStruct((rows // 2, cols), F32)],
        **params(12, 1.6),
    )(me.reshape(1), *parts)


def gather_rows(me, pieces, whole):
    part = pieces[0].shape[0] // 2
    for k, piece in zip((0, *HOPS), pieces):
        row = lax.rem(me[0] + 4 - k, 4) * part
        whole[pl.ds(pl.multiple_of(row, part), part), :] = piece[:part, :]
        whole[pl.ds(pl.multiple_of(row + 4 * part, part), part), :] = piece[part:, :]


def add_kernel(*refs):
    *parts, out = refs
    total = parts[0][...].astype(F32)
    for part in parts[1:]:
        total = total + part[...].astype(F32)
    out[...] = total.astype(out.dtype)


def add(dtype, *parts, us=0.1):
    return pl.pallas_call(
        add_kernel,
        in_specs=[VMEM] * len(parts),
        out_specs=VMEM,
        out_shape=jax.ShapeDtypeStruct(parts[0].shape, dtype),
        **params(8, us),
    )(*parts)


def pack_kernel(e1, e2, e3, up, down):
    rows = e1.shape[0]
    half = rows // 2
    for n, (eig, dst) in enumerate(((e1, up), (e3, down))):
        dst[:rows, :] = eig[...]
        dst[rows:, :] = e2[n * half : (n + 1) * half, :]


def pack(e1, e2, e3):
    rows, cols = e1.shape
    return pl.pallas_call(
        pack_kernel,
        in_specs=[VMEM] * 3,
        out_specs=[VMEM] * 2,
        out_shape=[jax.ShapeDtypeStruct((rows * 3 // 2, cols), e1.dtype)] * 2,
        **params(12, 0.2),
    )(e1, e2, e3)


def join_kernel(at, mine, other, whole):
    part = mine.shape[0]
    whole[pl.ds(pl.multiple_of(at[0] * part, part), part), :] = mine[...]
    whole[pl.ds(pl.multiple_of((1 - at[0]) * part, part), part), :] = other[...]


def join(me, mine, other):
    return pl.pallas_call(
        join_kernel,
        in_specs=[SMEM, VMEM, VMEM],
        out_specs=VMEM,
        out_shape=jax.ShapeDtypeStruct((2 * mine.shape[0], mine.shape[1]), mine.dtype),
        **params(8, 0.1),
    )(me.reshape(1), mine, other)


def onward_kernel(n, eig, rot_in, out):
    part = rot_in.shape[0] // 2
    out[:part, :] = rot_in[n * part : (n + 1) * part, :]
    out[part:, :] = eig[eig.shape[0] - out.shape[0] + part :, :]


def onward(n, eig, rot_in):
    rows = eig.shape[0] // 3 + rot_in.shape[0] // 2
    return pl.pallas_call(
        functools.partial(onward_kernel, n),
        in_specs=[VMEM] * 2,
        out_specs=VMEM,
        out_shape=jax.ShapeDtypeStruct((rows, eig.shape[1]), eig.dtype),
        **params(8, 0.1),
    )(eig, rot_in)


def score_kernel(me, pick, grid, *refs):
    pieces, eig_own, in_own, low, in_low, high, in_high, far_low, far_high = refs[:4], *refs[4:12]
    out, rot, rot_t, ti_t, eig_far, in_far = refs[12:]
    gather_rows(me, pieces, rot)
    width = eig_own.shape[0]
    part = in_own.shape[0] // 2
    in_far[:part, :] = far_low[:part, :]
    in_far[part:, :] = far_high[:part, :]
    eig_far[: width // 2, :] = far_low[part:, :]
    eig_far[width // 2 :, :] = far_high[part:, :]
    eigs = [eig_own, low.at[:width, :], high.at[:width, :], eig_far]
    ins = [in_own, in_low, in_high, in_far]
    for n in range(4):
        ti_t[n] = ins[n][256:, :].T
    for n in range(rot.shape[1] // 128):
        rot_t[n * 128 : (n + 1) * 128, :] = rot[:, n * 128 : (n + 1) * 128].T
    damp = [grid[pick[s]] for s in range(2)]
    weights = [None, None]
    for k in range(4):
        diag = eigs[k][...].astype(F32)
        for s in range(2):
            tokens = slice(s * 128, (s + 1) * 128)
            rotated = jnp.dot(rot_t[:, tokens], ins[k][tokens, :], preferred_element_type=F32)
            precond = (rotated / (diag + damp[s])).astype(BF)
            w = jnp.dot(precond, ti_t[k], preferred_element_type=F32)
            weights[s] = w if weights[s] is None else weights[s] + w
    train = rot_t[:, 256:].astype(F32)
    both = jnp.concatenate([jnp.sum(w * train, axis=0, keepdims=True) for w in weights], axis=0) * SCALE
    out[...] = jnp.broadcast_to(both[None], out.shape)


def score(me, pick, grid, pieces, eig, rot_in, messages):
    tokens, cols = pieces[0].shape
    return pl.pallas_call(
        score_kernel,
        in_specs=[SMEM] * 3 + [VMEM] * 12,
        out_specs=VMEM,
        out_shape=jax.ShapeDtypeStruct((16, 2, 256), F32),
        scratch_shapes=[
            pltpu.VMEM((4 * tokens, cols), BF),
            pltpu.VMEM((cols, 4 * tokens), BF),
            pltpu.VMEM((4, 256, 256), BF),
            pltpu.VMEM(eig.shape, BF),
            pltpu.VMEM(rot_in.shape, BF),
        ],
        **params(24, 3),
    )(me.reshape(1), pick, grid, *pieces, eig, rot_in, *messages)


def tie(value, *after):
    return lax.optimization_barrier((value, *after))[0]


def swap(value, axis, bit):
    size = 2 if axis in ("c", "zh") else 4
    return lax.ppermute(value, axis, [(i, i ^ bit) for i in range(size)])


def body(acts, out_grads, train_acts, train_grads, basis_in, basis_out, eig, grid, pick):
    y, x, c = lax.axis_index("y"), lax.axis_index("x"), lax.axis_index("c").astype(jnp.int32)
    first = jnp.where(c == 0, x, y).astype(jnp.int32)
    second = jnp.where(c == 0, y, x).astype(jnp.int32)
    width = basis_out.shape[1] // 4

    grads = (out_grads, train_grads)
    two_q, two_t, mine, other = open_mm(first, c, grads, basis_out, (acts, train_acts), basis_in, width)
    relay_q, relay_t = move(two_q, FIRST[1]), move(two_t, FIRST[3])
    in_chip = add(F32, mine, swap(other, "c", 1))
    up_q, up_t, down_q, down_t = lead_mm(*grads, basis_out, tie(first, two_q), (1, 3), width)
    from_down_t, from_up_q = move(up_t, FIRST[1]), move(down_q, FIRST[3])
    in_half = add(F32, in_chip, swap(in_chip, "zl", 1))
    up_q, down_t = add(BF, up_q, relay_q), add(BF, down_t, relay_t)
    from_down_q, from_up_t = move(up_q, FIRST[1]), move(down_t, FIRST[3])
    eig_own, *eigs = pick_blocks(eig, tie(first, up_q), width)
    up, down = pack(*eigs)
    low = move(tie(up, from_down_t, from_up_q), FIRST[1])
    high = move(tie(down, from_down_t, from_up_q), FIRST[3])
    own_q, own_t = block_mm(*grads, basis_out, tie(first, up_q, down_t), (0,), width, (F32,))
    far_half = swap(add(BF, in_half), "zl", 2)

    *send, keep = sum_blocks(second, own_q, own_t, from_down_q, from_up_q, from_down_t, from_up_t)
    got = [move(v, SECOND[k]) for k, v in zip(HOPS, send)]
    in_half = add(BF, in_half, tie(far_half, send[0]))
    rot_in = join(c, in_half, swap(in_half, "c", 1))
    in_low, in_high = move(rot_in, FIRST[1]), move(rot_in, FIRST[3])
    total = add(F32, keep, *got, us=8)
    near = add(BF, total)
    up, down = onward(0, low, in_low), onward(1, high, in_high)
    messages = low, in_low, high, in_high, move(up, FIRST[1]), move(down, FIRST[3])
    total = add(BF, total, swap(near, "zh", 1), us=4)
    pieces = [total] + [move(total, SECOND[k]) for k in HOPS]
    part = score(second, pick, grid, pieces, eig_own, rot_in, messages)

    over = jnp.sum(lax.all_to_all(part, ("zh", "zl", "c"), 0, 0, tiled=True), axis=0)
    over = jnp.broadcast_to(over[None], (16, *over.shape))
    return jnp.sum(lax.all_to_all(over, ("y", "x"), 0, 0, tiled=True), axis=0)


def solution(mesh):
    fine = Mesh(mesh.devices.reshape(SIZES), ALL)
    aa, ga = ("y", "x", "zh"), ("zl", "c")
    return jax.shard_map(
        body,
        mesh=fine,
        in_specs=(
            P(None, ga),
            P(None, aa),
            P(None, ga),
            P(None, aa),
            P(ga, aa),
            P(aa, ga),
            P(ga, aa),
            P(),
            P(),
        ),
        out_specs=P(),
        check_vma=False,
    )
```

```python
import functools
import itertools
import math

import jax
import jax.numpy as jnp
from jax import lax
from jax.experimental import pallas as pl
from jax.experimental.pallas import tpu as pltpu
from jax.sharding import Mesh, PartitionSpec as P

D_IN = 8192
D_OUT = 28672
SIZES = (4, 4, 2, 4, 2)
ALL = ("y", "x", "zh", "zl", "c")
SCALE = 1.0 / math.sqrt(D_IN * D_OUT)
BF = jnp.bfloat16
F32 = jnp.float32
MIB = 1024 * 1024


def flat(place):
    n = 0
    for size, at in zip(SIZES, place):
        n = n * size + at
    return n


def shift(k, first):
    pairs = []
    for y, x, zh, zl, c in itertools.product(*(range(s) for s in SIZES)):
        if (c == 0) == first:
            to = (y, (x + k) % 4, zh, zl, c)
        else:
            to = ((y + k) % 4, x, zh, zl, c)
        pairs.append((flat((y, x, zh, zl, c)), flat(to)))
    return pairs


FIRST = {k: shift(k, True) for k in (1, 2, 3)}
SECOND = {k: shift(k, False) for k in (1, 2, 3)}
HOPS = (2, 1, 3)


def move(value, pairs):
    return lax.ppermute(value, ALL, pairs)


def params(mib, us):
    return {
        "compiler_params": pltpu.CompilerParams(vmem_limit_bytes=mib * MIB),
        "cost_estimate": pl.CostEstimate(flops=int(us * 1.15e9), bytes_accessed=0, transcendentals=0),
    }


SMEM = pl.BlockSpec(memory_space=pltpu.SMEM)
VMEM = pl.BlockSpec(memory_space=pltpu.VMEM)


def lead_kernel(hops, at, q_hbm, t_hbm, b_hbm, *refs):
    outs, (q, t, b, sems) = refs[: 2 * len(hops)], refs[2 * len(hops) :]
    width = outs[0].shape[1]
    loads = [pltpu.make_async_copy(q_hbm, q, sems.at[0]), pltpu.make_async_copy(t_hbm, t, sems.at[1])]
    for n, k in enumerate(hops):
        cols = pl.ds(pl.multiple_of(lax.rem(at[0] + k, 4) * width, width), width)
        loads.append(pltpu.make_async_copy(b_hbm.at[:, cols], b.at[n], sems.at[2 + n]))
    for n in (0, 2, 1, *range(3, len(loads))):
        loads[n].start()
    for n in range(len(hops)):
        loads[2 + n].wait()
        for m, rows in enumerate((q, t)):
            if n == 0:
                loads[m].wait()
            dst = outs[2 * n + m]
            dst[...] = jnp.dot(rows[...], b[n], preferred_element_type=F32).astype(dst.dtype)


def lead_mm(q, t, basis, me, hops, width):
    rows, depth = q.shape
    hbm = pl.BlockSpec(memory_space=pltpu.HBM)
    return pl.pallas_call(
        functools.partial(lead_kernel, hops),
        in_specs=[SMEM, hbm, hbm, hbm],
        out_specs=[VMEM] * (2 * len(hops)),
        out_shape=[jax.ShapeDtypeStruct((rows, width), BF)] * (2 * len(hops)),
        scratch_shapes=[
            pltpu.VMEM((rows, depth), BF),
            pltpu.VMEM((rows, depth), BF),
            pltpu.VMEM((len(hops), depth, width), BF),
            pltpu.SemaphoreType.DMA((2 + len(hops),)),
        ],
        **params(58, 5),
    )(me.reshape(1), q, t, basis)


def open_kernel(at, core_at, q_hbm, t_hbm, b_hbm, aq_hbm, at_hbm, bi_hbm, oq, ot, mine, other, q, t, b, aq, ta, bi, sems):
    width = oq.shape[1]
    cols = pl.ds(pl.multiple_of(lax.rem(at[0] + 2, 4) * width, width), width)
    pairs = ((aq_hbm, aq), (at_hbm, ta), (bi_hbm, bi), (q_hbm, q), (b_hbm.at[:, cols], b), (t_hbm, t))
    loads = [pltpu.make_async_copy(src, dst, sems.at[n]) for n, (src, dst) in enumerate(pairs)]
    for load in loads:
        load.start()
    for load in loads[:3]:
        load.wait()
    for core in range(2):

        @pl.when(core_at[0] == core)
        def _():
            mine[...] = jnp.dot((aq, ta)[core][...], bi[...], preferred_element_type=F32)
            other[...] = jnp.dot((ta, aq)[core][...], bi[...], preferred_element_type=F32)

    loads[3].wait()
    loads[4].wait()
    oq[...] = jnp.dot(q[...], b[...], preferred_element_type=F32).astype(oq.dtype)
    loads[5].wait()
    ot[...] = jnp.dot(t[...], b[...], preferred_element_type=F32).astype(ot.dtype)


def open_mm(first, core, grads, basis_out, acts, basis_in, width):
    (rows, depth), (in_depth, in_width) = grads[0].shape, basis_in.shape
    hbm = pl.BlockSpec(memory_space=pltpu.HBM)
    return pl.pallas_call(
        open_kernel,
        in_specs=[SMEM] * 2 + [hbm] * 6,
        out_specs=[VMEM] * 4,
        out_shape=[jax.ShapeDtypeStruct((rows, width), BF)] * 2 + [jax.ShapeDtypeStruct((rows, in_width), F32)] * 2,
        scratch_shapes=[
            pltpu.VMEM((rows, depth), BF),
            pltpu.VMEM((rows, depth), BF),
            pltpu.VMEM((depth, width), BF),
            pltpu.VMEM((rows, in_depth), BF),
            pltpu.VMEM((rows, in_depth), BF),
            pltpu.VMEM((in_depth, in_width), BF),
            pltpu.SemaphoreType.DMA((6,)),
        ],
        **params(58, 4.5),
    )(first.reshape(1), core.reshape(1), *grads, basis_out, *acts, basis_in)


def mm_kernel(hops, at, q_ref, t_ref, b_ref, *outs):
    width = outs[0].shape[1]
    blocks = b_ref.shape[1] // width
    for n, k in enumerate(hops):
        if blocks == 1:
            basis = b_ref[...]
        else:
            basis = b_ref[:, pl.ds(pl.multiple_of(lax.rem(at[0] + k, blocks) * width, width), width)]
        for ref, dst in ((q_ref, outs[2 * n]), (t_ref, outs[2 * n + 1])):
            dst[...] = jnp.dot(ref[...], basis, preferred_element_type=F32).astype(dst.dtype)


def block_mm(q, t, basis, me, hops, width, dtypes):
    return pl.pallas_call(
        functools.partial(mm_kernel, hops),
        in_specs=[SMEM, VMEM, VMEM, VMEM],
        out_specs=[VMEM] * (2 * len(hops)),
        out_shape=[jax.ShapeDtypeStruct((q.shape[0], width), d) for d in dtypes for _ in range(2)],
        **params(20, 4),
    )(me.reshape(1), q, t, basis)


def pick_kernel(at, *refs):
    half = len(refs) // 2
    for src, dst in zip(refs[:half], refs[half:]):
        dst[...] = src[...]


def pick_blocks(array, me, rows):
    cols = array.shape[1]
    return pl.pallas_call(
        pick_kernel,
        grid_spec=pltpu.PrefetchScalarGridSpec(
            num_scalar_prefetch=1,
            grid=(1,),
            in_specs=[
                pl.BlockSpec((rows, cols), lambda i, at, k=k: (lax.rem(at[0] + k, 4), 0)) for k in range(4)
            ],
            out_specs=[pl.BlockSpec((rows, cols), lambda i, at: (0, 0))] * 4,
        ),
        out_shape=[jax.ShapeDtypeStruct((rows, cols), array.dtype)] * 4,
        **params(16, 1.2),
    )(me.reshape(1), array, array, array, array)


def sum_kernel(at, own_q, own_t, q1, q2, t1, t2, o2, o1, o3, keep):
    part = keep.shape[0] // 2
    for hop, dst in ((2, o2), (1, o1), (3, o3), (0, keep)):
        rows = pl.ds(pl.multiple_of(lax.rem(at[0] + hop, 4) * part, part), part)
        for n, (a, b, c) in enumerate(((own_q, q1, q2), (own_t, t1, t2))):
            total = a[rows, :] + b[rows, :].astype(F32) + c[rows, :].astype(F32)
            dst[n * part : (n + 1) * part, :] = total.astype(dst.dtype)


def sum_blocks(me, *parts):
    rows, cols = parts[0].shape
    small = jax.ShapeDtypeStruct((rows // 2, cols), BF)
    return pl.pallas_call(
        sum_kernel,
        in_specs=[SMEM] + [VMEM] * 6,
        out_specs=[VMEM] * 4,
        out_shape=[small, small, small, jax.ShapeDtypeStruct((rows // 2, cols), F32)],
        **params(12, 1.6),
    )(me.reshape(1), *parts)


def relay_kernel(up, from_up, down, from_down, up_out, down_out):
    up_out[...] = (up[...].astype(F32) + from_up[...].astype(F32)).astype(BF)
    down_out[...] = (down[...].astype(F32) + from_down[...].astype(F32)).astype(BF)


def relay(*parts):
    return pl.pallas_call(
        relay_kernel,
        in_specs=[VMEM] * 4,
        out_specs=[VMEM] * 2,
        out_shape=[jax.ShapeDtypeStruct(parts[0].shape, BF)] * 2,
        **params(8, 0.1),
    )(*parts)


def gather_rows(me, pieces, whole):
    part = pieces[0].shape[0] // 2
    for k, piece in zip((0, *HOPS), pieces):
        row = lax.rem(me[0] + 4 - k, 4) * part
        whole[pl.ds(pl.multiple_of(row, part), part), :] = piece[:part, :]
        whole[pl.ds(pl.multiple_of(row + 4 * part, part), part), :] = piece[part:, :]


def add_kernel(*refs):
    *parts, out = refs
    total = parts[0][...].astype(F32)
    for part in parts[1:]:
        total = total + part[...].astype(F32)
    out[...] = total.astype(out.dtype)


def add(dtype, *parts, us=0.1):
    return pl.pallas_call(
        add_kernel,
        in_specs=[VMEM] * len(parts),
        out_specs=VMEM,
        out_shape=jax.ShapeDtypeStruct(parts[0].shape, dtype),
        **params(8, us),
    )(*parts)


def pack_kernel(e1, e2, e3, up, down):
    rows = e1.shape[0]
    half = rows // 2
    for n, (eig, dst) in enumerate(((e1, up), (e3, down))):
        dst[:rows, :] = eig[...]
        dst[rows:, :] = e2[n * half : (n + 1) * half, :]


def pack(e1, e2, e3):
    rows, cols = e1.shape
    return pl.pallas_call(
        pack_kernel,
        in_specs=[VMEM] * 3,
        out_specs=[VMEM] * 2,
        out_shape=[jax.ShapeDtypeStruct((rows * 3 // 2, cols), e1.dtype)] * 2,
        **params(12, 0.2),
    )(e1, e2, e3)


def join_kernel(at, mine, other, whole):
    part = mine.shape[0]
    whole[pl.ds(pl.multiple_of(at[0] * part, part), part), :] = mine[...]
    whole[pl.ds(pl.multiple_of((1 - at[0]) * part, part), part), :] = other[...]


def join(me, mine, other):
    return pl.pallas_call(
        join_kernel,
        in_specs=[SMEM, VMEM, VMEM],
        out_specs=VMEM,
        out_shape=jax.ShapeDtypeStruct((2 * mine.shape[0], mine.shape[1]), mine.dtype),
        **params(8, 0.1),
    )(me.reshape(1), mine, other)


def onward_kernel(n, eig, rot_in, out):
    part = rot_in.shape[0] // 2
    out[:part, :] = rot_in[n * part : (n + 1) * part, :]
    out[part:, :] = eig[eig.shape[0] - out.shape[0] + part :, :]


def onward(n, eig, rot_in):
    rows = eig.shape[0] // 3 + rot_in.shape[0] // 2
    return pl.pallas_call(
        functools.partial(onward_kernel, n),
        in_specs=[VMEM] * 2,
        out_specs=VMEM,
        out_shape=jax.ShapeDtypeStruct((rows, eig.shape[1]), eig.dtype),
        **params(8, 0.1),
    )(eig, rot_in)


def score_kernel(me, pick, grid, *refs):
    pieces, eig_own, in_own, low, in_low, high, in_high, far_low, far_high = refs[:4], *refs[4:12]
    out, rot, rot_t, ti_t, eig_far, in_far = refs[12:]
    gather_rows(me, pieces, rot)
    width = eig_own.shape[0]
    part = in_own.shape[0] // 2
    in_far[:part, :] = far_low[:part, :]
    in_far[part:, :] = far_high[:part, :]
    eig_far[: width // 2, :] = far_low[part:, :]
    eig_far[width // 2 :, :] = far_high[part:, :]
    eigs = [eig_own, low.at[:width, :], high.at[:width, :], eig_far]
    ins = [in_own, in_low, in_high, in_far]
    for n in range(4):
        ti_t[n] = ins[n][256:, :].T
    for n in range(rot.shape[1] // 128):
        rot_t[n * 128 : (n + 1) * 128, :] = rot[:, n * 128 : (n + 1) * 128].T
    damp = [grid[pick[s]] for s in range(2)]
    weights = [None, None]
    for k in range(4):
        diag = eigs[k][...].astype(F32)
        for s in range(2):
            tokens = slice(s * 128, (s + 1) * 128)
            rotated = jnp.dot(rot_t[:, tokens], ins[k][tokens, :], preferred_element_type=F32)
            precond = (rotated / (diag + damp[s])).astype(BF)
            w = jnp.dot(precond, ti_t[k], preferred_element_type=F32)
            weights[s] = w if weights[s] is None else weights[s] + w
    train = rot_t[:, 256:].astype(F32)
    both = jnp.concatenate([jnp.sum(w * train, axis=0, keepdims=True) for w in weights], axis=0) * SCALE
    out[...] = jnp.broadcast_to(both[None], out.shape)


def score(me, pick, grid, pieces, eig, rot_in, messages):
    tokens, cols = pieces[0].shape
    return pl.pallas_call(
        score_kernel,
        in_specs=[SMEM] * 3 + [VMEM] * 12,
        out_specs=VMEM,
        out_shape=jax.ShapeDtypeStruct((16, 2, 256), F32),
        scratch_shapes=[
            pltpu.VMEM((4 * tokens, cols), BF),
            pltpu.VMEM((cols, 4 * tokens), BF),
            pltpu.VMEM((4, 256, 256), BF),
            pltpu.VMEM(eig.shape, BF),
            pltpu.VMEM(rot_in.shape, BF),
        ],
        **params(24, 3),
    )(me.reshape(1), pick, grid, *pieces, eig, rot_in, *messages)


def tie(value, *after):
    return lax.optimization_barrier((value, *after))[0]


def swap(value, axis, bit):
    size = 2 if axis in ("c", "zh") else 4
    return lax.ppermute(value, axis, [(i, i ^ bit) for i in range(size)])


def body(acts, out_grads, train_acts, train_grads, basis_in, basis_out, eig, grid, pick):
    y, x, c = lax.axis_index("y"), lax.axis_index("x"), lax.axis_index("c").astype(jnp.int32)
    first = jnp.where(c == 0, x, y).astype(jnp.int32)
    second = jnp.where(c == 0, y, x).astype(jnp.int32)
    width = basis_out.shape[1] // 4

    grads = (out_grads, train_grads)
    two_q, two_t, mine, other = open_mm(first, c, grads, basis_out, (acts, train_acts), basis_in, width)
    relay_q, relay_t = move(two_q, FIRST[1]), move(two_t, FIRST[3])
    in_chip = add(F32, mine, swap(other, "c", 1))
    up_q, up_t, down_q, down_t = lead_mm(*grads, basis_out, tie(first, two_q), (1, 3), width)
    from_down_t, from_up_q = move(up_t, FIRST[1]), move(down_q, FIRST[3])
    in_half = add(F32, in_chip, swap(in_chip, "zl", 1))
    up_q, down_t = relay(up_q, relay_q, down_t, relay_t)
    from_down_q, from_up_t = move(up_q, FIRST[1]), move(down_t, FIRST[3])
    eig_own, *eigs = pick_blocks(eig, tie(first, up_q), width)
    up, down = pack(*eigs)
    low = move(tie(up, from_down_t, from_up_q), FIRST[1])
    high = move(tie(down, from_down_t, from_up_q), FIRST[3])
    own_q, own_t = block_mm(*grads, basis_out, tie(first, up_q, down_t), (0,), width, (F32,))
    far_half = swap(add(BF, in_half), "zl", 2)

    *send, keep = sum_blocks(second, own_q, own_t, from_down_q, from_up_q, from_down_t, from_up_t)
    got = [move(v, SECOND[k]) for k, v in zip(HOPS, send)]
    in_half = add(BF, in_half, tie(far_half, send[0]))
    rot_in = join(c, in_half, swap(in_half, "c", 1))
    in_low, in_high = move(rot_in, FIRST[1]), move(rot_in, FIRST[3])
    total = add(F32, keep, *got, us=8)
    near = add(BF, total)
    up, down = onward(0, low, in_low), onward(1, high, in_high)
    messages = low, in_low, high, in_high, move(up, FIRST[1]), move(down, FIRST[3])
    total = add(BF, total, swap(near, "zh", 1), us=4)
    pieces = [total] + [move(total, SECOND[k]) for k in HOPS]
    part = score(second, pick, grid, pieces, eig_own, rot_in, messages)

    over = jnp.sum(lax.all_to_all(part, ("zh", "zl", "c"), 0, 0, tiled=True), axis=0)
    over = jnp.broadcast_to(over[None], (16, *over.shape))
    return jnp.sum(lax.all_to_all(over, ("y", "x"), 0, 0, tiled=True), axis=0)


def solution(mesh):
    fine = Mesh(mesh.devices.reshape(SIZES), ALL)
    aa, ga = ("y", "x", "zh"), ("zl", "c")
    return jax.shard_map(
        body,
        mesh=fine,
        in_specs=(
            P(None, ga),
            P(None, aa),
            P(None, ga),
            P(None, aa),
            P(ga, aa),
            P(aa, ga),
            P(ga, aa),
            P(),
            P(),
        ),
        out_specs=P(),
        check_vma=False,
    )
```
